256 devices in a mesh: serve: 128 (over y, x, z), rep: 2 (over core).
Axes of the slice: x: 4, y: 4, z: 8, core: 2. Of those that a mesh axis runs over, the one named last changes fastest.
Arguments:
- history: bfloat16 [131072, 1024], P(('serve', 'rep')), may hold values from -6 to 6
- candidates: bfloat16 [65536, 1024], P(('serve', 'rep')), may hold values from -6 to 6
- cand_user: int32 [65536, 1], P(('serve', 'rep')), may hold values from 0 to 127; in each aligned block of 256 rows (0 to 255, 256 to 511, ...) at most 4 rows name the same one
- hist_len: int32 [128], P('serve'), may hold values from 1 to 1024, as said below
- w_uvqk: bfloat16 [1024, 4096], replicated, may hold values from -0.1875 to 0.1875
- w_out: bfloat16 [1024, 1024], replicated, may hold values from -0.1875 to 0.1875
Outputs:
- scored: bfloat16 [65536, 1024], P(('serve', 'rep'))
The draws below stay inside these ranges and needn't reach their ends.
Inputs may be any that keep to these rules, and one draw needn't show every extreme that they name: `cand_user`: in each aligned block of 256 rows no user is named more than 4 times, a bound that some block reaches. `hist_len`: some user has exactly 1024 valid events.
All inputs are finite; a program needn't handle non-finite values.
Results may differ from the reference program's by a relative error of at most 0.007.
Values may be sent and summed in bfloat16 or wider, within the bound.
No kernel may reach another device: no remote copies, remote signals or barrier semaphores. Data moves between devices by JAX's collectives and lax.ppermute only.
A program may use at most 64 MiB of HBM per device.

```python
import math
import jax
import jax.numpy as jnp
import numpy as np
from jax import lax

D = 1024
HEADS = 8
CAND_DEV = 256
USERS = 128
HIST = 1024
NC = 65536
CAP = 4
N_SERVE = 128
N_REP = 2


def draw_hist_len(key, part):
    key = jax.random.fold_in(key, 11)
    first_key, second_key = jax.random.split(key)
    lengths = jax.random.randint(first_key, (USERS,), 1, HIST + 1, dtype=jnp.int32)
    longest = jax.random.randint(second_key, (), 0, USERS, dtype=jnp.int32)
    return lengths.at[longest].set(HIST)


def block_levels(rng, dims, cuts, smallest, high):
    gain, own = 1.0, jax.random.fold_in(rng, 6)
    for dim, parts in cuts:
        draws = jnp.exp(jax.random.uniform(jax.random.fold_in(own, dim), (parts,), jnp.float32, smallest / len(cuts), high / len(cuts)))
        gain = gain * jnp.repeat(draws, dims[dim] // parts).reshape([-1 if axis == dim else 1 for axis in range(len(dims))])
    return gain


def shared_out(own_key, own, number, rows, amount, top, bound, lean):
    order = jax.random.permutation(own_key, amount)
    crowded, common = load_shares(amount, rows * top, bound, lean, True), load_shares(amount, rows * top, bound, lean, False)
    places = jnp.arange(amount)

    def named(sizes, turn):
        used = int((sizes > 0).sum())
        fixed = max(1, used // 4)
        shifted = fixed + (places - fixed + turn * (used - fixed)) % max(1, amount - fixed)
        return jnp.zeros((amount,), jnp.int32).at[order[jnp.where(places < fixed, places, shifted)]].set(jnp.asarray(sizes, jnp.int32))

    sizes = jnp.where(number % 4 == 0, named(crowded, number // 4), named(common, number - number // 4 - 1))
    mixed = jax.random.permutation(jax.random.fold_in(own, 3), amount)
    donor, receiver = mixed[0:amount // 2 * 2:2], mixed[1:amount // 2 * 2:2]
    room = jnp.minimum(sizes[donor] - 1, bound - sizes[receiver]) // 2
    room = jnp.where((donor == order[0]) | (receiver == order[0]) | (sizes[receiver] == 0), 0, jnp.maximum(room, 0))
    shifted = jax.random.randint(jax.random.fold_in(own, 4), (amount // 2,), 0, 1 << 20) % (room + 1)
    sizes = sizes.at[donor].add(-shifted).at[receiver].add(shifted)
    items = jnp.searchsorted(jnp.cumsum(sizes), jnp.arange(rows * top), side="right").astype(jnp.int32)
    grid = items.reshape(top, rows).T
    grid = grid[jax.random.permutation(jax.random.fold_in(own, 1), rows)]
    turn = jax.random.randint(jax.random.fold_in(own, 2), (rows, 1), 0, top)
    return jnp.take_along_axis(grid, (jnp.arange(top)[None, :] + turn) % top, axis=1)


def load_shares(amount, total, most, slope, full):
    weights = [(1 << 20) // math.isqrt(standing ** slope) + 1 for standing in range(1, amount + 1)]
    largest = most if full else min(most, max(-(-total // amount), total * weights[0] // sum(weights)))
    least = 1 if total - largest >= amount - 1 else 0
    given, rest = [largest] + [least] * (amount - 1), total - largest - least * (amount - 1)
    while rest > 0:
        free = [i for i in range(1, amount) if given[i] < largest] or [i for i in range(1, amount) if given[i] < most]
        pool, budget = sum([weights[i] for i in free]), rest
        for i in free:
            more = min(most - given[i], max(1, budget * weights[i] // pool), rest)
            given[i] = given[i] + more
            rest = rest - more
    return np.array(given)


def normal_values(own_key, dims, deviation, limit, cuts=(), held_as=jnp.bfloat16):
    drawn = jax.random.normal(own_key, dims, jnp.float32) * deviation
    if len(cuts) > 0:
        drawn = block_levels(own_key, dims, cuts, -0.22, 0.18) * drawn
    return jnp.clip(drawn, min=-limit, max=limit).astype(held_as)


def setup_inputs(seed: int = 0) -> dict:
    streams_of = jax.random.split(jax.random.key(seed), 7)
    history = normal_values(streams_of[0], (USERS * HIST, D), 1.0, 6.0, ((0, 256),))
    candidates = normal_values(streams_of[1], (NC, D), 1.0, 6.0, ((0, 256),))
    cand_user_keys = jax.random.split(jax.random.fold_in(streams_of[2], 1), NC // CAND_DEV)
    cand_user_turns = jax.random.permutation(jax.random.fold_in(streams_of[2], 3), NC // CAND_DEV)
    cand_user = jax.vmap(lambda own, number: shared_out(jax.random.fold_in(streams_of[2], 2), own, number, CAND_DEV, USERS, 1, CAP, 2))(cand_user_keys, cand_user_turns).reshape((NC, 1))
    hist_len = draw_hist_len(jax.random.fold_in(streams_of[6], 71), 0)
    w_uvqk = normal_values(streams_of[4], (D, 4 * D), D ** -0.5, 0.1875)
    w_out = normal_values(streams_of[5], (D, D), D ** -0.5, 0.1875)
    return {"history": history, "candidates": candidates, "cand_user": cand_user, "hist_len": hist_len, "w_uvqk": w_uvqk, "w_out": w_out}


def silu_rows(matrix, weight):
    return jax.nn.silu(jnp.dot(matrix, weight, preferred_element_type=jnp.float32)).astype(jnp.bfloat16)

def history_attention(queries, keys_vals, length):
    feature_width = queries.shape[1]
    head_size = feature_width // HEADS
    key_rows = keys_vals[:, :feature_width].reshape(-1, HEADS, head_size).astype(jnp.float32)
    value_rows = keys_vals[:, feature_width:].reshape(-1, HEADS, head_size).astype(jnp.float32)
    query_rows = queries.reshape(-1, HEADS, head_size).astype(jnp.float32)
    scores = jnp.einsum('ihd,jhd->hij', query_rows, key_rows) / math.sqrt(head_size)
    key_mask = (jnp.arange(key_rows.shape[0], dtype=jnp.int32) < length).astype(jnp.float32)
    weights = (jax.nn.silu(scores) * key_mask[None, None, :]).astype(jnp.bfloat16)
    weights = lax.optimization_barrier(weights).astype(jnp.float32)
    result = jnp.einsum('hij,jhd->ihd', weights, value_rows)
    return result.reshape(-1, feature_width).astype(jnp.bfloat16)

def finish(candidates, projected, history_part, w_out):
    feature_width = candidates.shape[1]
    head_size = feature_width // HEADS
    gate_rows = projected[:, :feature_width].astype(jnp.float32)
    value_rows = projected[:, feature_width:2 * feature_width].reshape(-1, HEADS, head_size).astype(jnp.float32)
    query_rows = projected[:, 2 * feature_width:3 * feature_width].reshape(-1, HEADS, head_size).astype(jnp.float32)
    key_rows = projected[:, 3 * feature_width:].reshape(-1, HEADS, head_size).astype(jnp.float32)
    self_scores = lax.optimization_barrier(jnp.sum(query_rows * key_rows, -1)) / math.sqrt(head_size)
    self_term = (jax.nn.silu(self_scores)[:, :, None] * value_rows).reshape(-1, feature_width)
    attended = history_part.astype(jnp.float32) + self_term
    row_mean = lax.optimization_barrier(jnp.mean(attended, 1, keepdims=True))
    row_var = lax.optimization_barrier(jnp.mean(jnp.square(attended - row_mean), 1, keepdims=True))
    normed = ((attended - row_mean) * lax.rsqrt(row_var + 1e-05) * gate_rows).astype(jnp.bfloat16)
    output = candidates.astype(jnp.float32) + jnp.dot(normed, w_out, preferred_element_type=jnp.float32)
    return output.astype(jnp.bfloat16)

def reference(history, candidates, cand_user, hist_len, w_uvqk, w_out):
    feature_width = candidates.shape[1]
    w_kv = jnp.concatenate([w_uvqk[:, 3 * feature_width:], w_uvqk[:, feature_width:2 * feature_width]], 1)
    projected = silu_rows(candidates, w_uvqk)
    query_self = projected[:, 2 * feature_width:3 * feature_width]
    user_ids = cand_user[:, 0].astype(jnp.int32)
    sort_order = jnp.argsort(user_ids, stable=True).astype(jnp.int32)
    counts = lax.optimization_barrier(jnp.sum((user_ids[:, None] == jnp.arange(USERS, dtype=jnp.int32)[None, :]).astype(jnp.int32), 0))
    offsets = (jnp.cumsum(counts) - counts).astype(jnp.int32)
    window = N_SERVE * N_REP * CAP
    total_rows = candidates.shape[0]
    sorted_queries = jnp.concatenate([query_self[sort_order], jnp.zeros((window, feature_width), jnp.bfloat16)], 0)
    sorted_users = jnp.concatenate([user_ids[sort_order], jnp.full((window,), -1, jnp.int32)], 0)

    def visit_user(buffer, user_index):
        user_rows = lax.dynamic_slice_in_dim(history, (user_index * HIST).astype(jnp.int32), HIST, 0)
        keys_vals = silu_rows(user_rows, w_kv)
        start_row = offsets[user_index]
        block_queries = lax.dynamic_slice_in_dim(sorted_queries, start_row, window, 0)
        block_users = lax.dynamic_slice_in_dim(sorted_users, start_row, window, 0)
        partial_rows = history_attention(block_queries, keys_vals, hist_len[user_index])
        keep_rows = (block_users == user_index)[:, None]
        current = lax.dynamic_slice_in_dim(buffer, start_row, window, 0)
        buffer = lax.dynamic_update_slice_in_dim(buffer, jnp.where(keep_rows, partial_rows, current), start_row, 0)
        return (buffer, None)
    buffer = jnp.zeros((total_rows + window, feature_width), jnp.bfloat16)
    buffer, _ = lax.scan(visit_user, buffer, jnp.arange(USERS, dtype=jnp.int32))
    inverse = jnp.argsort(sort_order).astype(jnp.int32)
    history_part = buffer[:total_rows][inverse]
    return finish(candidates, projected, history_part, w_out)
```

```python
import functools
import math

import jax
import jax.numpy as jnp
from jax import lax
from jax.experimental import pallas as pl
from jax.experimental.pallas import tpu as pltpu
from jax.sharding import PartitionSpec as P

HEADS = 8
CAP = 4
BF16 = jnp.bfloat16
F32 = jnp.float32


def silu(x):
    y = 0.5 * x
    return y + y * jnp.tanh(y)


def dot(a, b):
    return jnp.dot(a, b, preferred_element_type=F32)


def weave(first, second):
    low = lax.broadcasted_iota(jnp.int32, first.shape, 1) < 4
    even = jnp.where(low, first, pltpu.roll(second, 4, 1))
    odd = jnp.where(low, pltpu.roll(first, 4, 1), second)
    return even, odd


def front_kernel(user_ref, cand_ref, w0_ref, w1_ref, out_ref, q0_ref, q1_ref, place_ref):
    rows, slots = place_ref.shape
    users = slots // CAP

    @pl.when(pl.program_id(0) == 0)
    def _():
        ids = user_ref[...]
        one_hot = jnp.where(ids == lax.broadcasted_iota(jnp.int32, (rows, users), 1), 1.0, 0.0)
        earlier = jnp.where(
            lax.broadcasted_iota(jnp.int32, (rows, rows), 1)
            < lax.broadcasted_iota(jnp.int32, (rows, rows), 0),
            1.0,
            0.0,
        )
        before = dot(earlier.astype(BF16), one_hot.astype(BF16))
        rank = jnp.sum(before * one_hot, 1, keepdims=True).astype(jnp.int32)
        slot = ids * CAP + rank
        place_ref[...] = jnp.where(
            slot == lax.broadcasted_iota(jnp.int32, (rows, slots), 1), 1.0, 0.0
        ).astype(BF16)

    place = place_ref[...]
    cand = cand_ref[...]
    parts = []
    for w_ref, q_ref in ((w0_ref, q0_ref), (w1_ref, q1_ref)):
        query = silu(dot(cand, w_ref[...])).astype(BF16)
        q_ref[...] = query
        moved = lax.dot_general(place, query, (((0,), (0,)), ((), ())), preferred_element_type=F32)
        parts.append(moved.reshape(slots // 8, 8, query.shape[1]))
    even, odd = weave(*parts)
    out_ref[:, 0] = even.astype(BF16)
    out_ref[:, 1] = odd.astype(BF16)


def front(cand_user, candidates, w_uvqk, users):
    rows, width = candidates.shape
    half = width // 2
    block = min(256, half)
    steps = half // block
    base = 2 * width // block
    slots = users * CAP
    return pl.pallas_call(
        front_kernel,
        grid=(steps,),
        in_specs=[
            pl.BlockSpec((rows, 1), lambda j: (0, 0)),
            pl.BlockSpec((rows, width), lambda j: (0, 0)),
            pl.BlockSpec((width, block), lambda j: (0, base + j)),
            pl.BlockSpec((width, block), lambda j: (0, base + steps + j)),
        ],
        out_specs=[
            pl.BlockSpec((slots // 8, 2, 8, block), lambda j: (0, 0, 0, j)),
            pl.BlockSpec((rows, block), lambda j: (0, j)),
            pl.BlockSpec((rows, block), lambda j: (0, j)),
            pl.BlockSpec((rows, slots), lambda j: (0, 0)),
        ],
        out_shape=[
            jax.ShapeDtypeStruct((slots // 8, 2, 8, half), BF16),
            jax.ShapeDtypeStruct((rows, half), BF16),
            jax.ShapeDtypeStruct((rows, half), BF16),
            jax.ShapeDtypeStruct((rows, slots), BF16),
        ],
        compiler_params=pltpu.CompilerParams(vmem_limit_bytes=40 << 20),
        cost_estimate=pl.CostEstimate(
            flops=2 * rows * width * (width + slots), bytes_accessed=5 << 20, transcendentals=rows * width
        ),
        name="front",
    )(cand_user, candidates, w_uvqk, w_uvqk)


def keys_vals_kernel(steps, info_ref, own_ref, other_ref, w_ref, out_ref):
    count = own_ref.shape[0]
    is_value = pl.program_id(0) >= steps
    weight = w_ref[...]
    for part, ref in enumerate((own_ref, other_ref)):
        start = jnp.where(info_ref[1] == part, 0, count)
        result = silu(dot(ref[...], weight))
        event = start + lax.broadcasted_iota(jnp.int32, result.shape, 0)
        keep = jnp.logical_or(jnp.logical_not(is_value), event < info_ref[0])
        out_ref[part * count : (part + 1) * count] = jnp.where(keep, result, 0.0).astype(BF16)


def keys_vals(info, own, other, w_uvqk):
    count, width = own.shape
    block = min(256, width)
    steps = width // block
    return pl.pallas_call(
        functools.partial(keys_vals_kernel, steps),
        grid=(2 * steps,),
        in_specs=[
            pl.BlockSpec(memory_space=pltpu.SMEM),
            pl.BlockSpec((count, width), lambda j: (0, 0)),
            pl.BlockSpec((count, width), lambda j: (0, 0)),
            pl.BlockSpec((width, block), lambda j: (0, jnp.where(j < steps, 3 * steps + j, j))),
        ],
        out_specs=pl.BlockSpec((2 * count, block), lambda j: (0, j)),
        out_shape=jax.ShapeDtypeStruct((2 * count, 2 * width), BF16),
        compiler_params=pltpu.CompilerParams(vmem_limit_bytes=40 << 20),
        cost_estimate=pl.CostEstimate(
            flops=8 * count * width * width, bytes_accessed=10 << 20, transcendentals=4 * count * width
        ),
        name="keys_vals",
    )(info, own, other, w_uvqk)


def attention_kernel(head_size, got_ref, key_ref, value_ref, out_ref, query_ref, result_ref):
    step = pl.program_id(0)
    steps = pl.num_programs(0)
    tiles, _, _, half = got_ref.shape
    slots = tiles * 8
    heads_half = half // head_size

    @pl.when(step == 0)
    def _():
        parts = weave(got_ref[:, 0].astype(F32), got_ref[:, 1].astype(F32))
        for index, part in enumerate(parts):
            rows = part.reshape(slots, half).astype(BF16)
            for head in range(heads_half):
                query_ref[index * heads_half + head] = rows[
                    :, head * head_size : (head + 1) * head_size
                ]

    scale = 0.5 / math.sqrt(head_size)
    chunk = min(256, slots)
    for start in range(0, slots, chunk):
        scores = lax.dot_general(
            query_ref[step, start : start + chunk],
            key_ref[...],
            (((1,), (1,)), ((), ())),
            preferred_element_type=F32,
        )
        y = scores * scale
        weights = (y + y * jnp.tanh(y)).astype(BF16)
        result_ref[step, start : start + chunk] = dot(weights, value_ref[...])

    @pl.when(step == steps - 1)
    def _():
        for head in range(heads_half):
            first = result_ref[head].reshape(tiles, 8, head_size)
            second = result_ref[heads_half + head].reshape(tiles, 8, head_size)
            even, odd = weave(first, second)
            columns = slice(head * head_size, (head + 1) * head_size)
            out_ref[:, 0, :, columns] = even.astype(BF16)
            out_ref[:, 1, :, columns] = odd.astype(BF16)


def attention(got, kv):
    tiles, _, _, half = got.shape
    slots = tiles * 8
    events = kv.shape[0]
    head_size = 2 * half // HEADS
    whole = pl.BlockSpec(got.shape, lambda h: (0, 0, 0, 0))
    return pl.pallas_call(
        functools.partial(attention_kernel, head_size),
        grid=(HEADS,),
        in_specs=[
            whole,
            pl.BlockSpec((events, head_size), lambda h: (0, h)),
            pl.BlockSpec((events, head_size), lambda h: (0, HEADS + h)),
        ],
        out_specs=whole,
        out_shape=jax.ShapeDtypeStruct(got.shape, BF16),
        scratch_shapes=[
            pltpu.VMEM((HEADS, slots, head_size), BF16),
            pltpu.VMEM((HEADS, slots, head_size), F32),
        ],
        compiler_params=pltpu.CompilerParams(vmem_limit_bytes=40 << 20),
        cost_estimate=pl.CostEstimate(
            flops=8 * slots * events * half,
            bytes_accessed=6 << 20,
            transcendentals=slots * events * HEADS,
        ),
        name="attention",
    )(got, kv, kv)


def own_kernel(head_size, cand_ref, query_ref, wg_ref, wv_ref, wk_ref, gate_ref, term_ref):
    cand = cand_ref[...]
    gate_ref[...] = silu(dot(cand, wg_ref[...])).astype(BF16)
    value = silu(dot(cand, wv_ref[...])).astype(BF16).astype(F32)
    key = silu(dot(cand, wk_ref[...])).astype(BF16).astype(F32)
    product = query_ref[...].astype(F32) * key
    for start in range(0, product.shape[1], head_size):
        columns = slice(start, start + head_size)
        score = jnp.sum(product[:, columns], 1, keepdims=True) / math.sqrt(head_size)
        term_ref[:, columns] = silu(score) * value[:, columns]


def own_part(candidates, query, w_uvqk, index):
    rows, width = candidates.shape
    half = width // 2
    block = min(256, half)
    steps = half // block
    full = width // block
    offset = index * steps
    return pl.pallas_call(
        functools.partial(own_kernel, width // HEADS),
        grid=(steps,),
        in_specs=[
            pl.BlockSpec((rows, width), lambda j: (0, 0)),
            pl.BlockSpec((rows, block), lambda j: (0, j)),
            pl.BlockSpec((width, block), lambda j: (0, offset + j)),
            pl.BlockSpec((width, block), lambda j: (0, full + offset + j)),
            pl.BlockSpec((width, block), lambda j: (0, 3 * full + offset + j)),
        ],
        out_specs=[
            pl.BlockSpec((rows, block), lambda j: (0, j)),
            pl.BlockSpec((rows, block), lambda j: (0, j)),
        ],
        out_shape=[
            jax.ShapeDtypeStruct((rows, half), BF16),
            jax.ShapeDtypeStruct((rows, half), F32),
        ],
        compiler_params=pltpu.CompilerParams(vmem_limit_bytes=40 << 20),
        cost_estimate=pl.CostEstimate(
            flops=6 * rows * width * half, bytes_accessed=5 << 20, transcendentals=3 * rows * half
        ),
        name="own_part",
    )(candidates, query, w_uvqk, w_uvqk, w_uvqk)


def tail_kernel(
    got_ref, place_ref, gate0_ref, gate1_ref, term0_ref, term1_ref, cand_ref, w_ref, out_ref, normed_ref
):
    tiles, _, _, half = got_ref.shape
    width = 2 * half

    @pl.when(pl.program_id(0) == 0)
    def _():
        place = place_ref[...]
        parts = weave(got_ref[:, 0].astype(F32), got_ref[:, 1].astype(F32))
        attended = []
        for part, term_ref in zip(parts, (term0_ref, term1_ref)):
            history = dot(place, part.reshape(tiles * 8, half).astype(BF16))
            attended.append(history + term_ref[...])
        mean = sum(jnp.sum(a, 1, keepdims=True) for a in attended) / width
        centred = [a - mean for a in attended]
        var = sum(jnp.sum(c * c, 1, keepdims=True) for c in centred) / width
        inverse = lax.rsqrt(var + 1e-05)
        for index, gate_ref in enumerate((gate0_ref, gate1_ref)):
            normed = centred[index] * inverse * gate_ref[...].astype(F32)
            normed_ref[:, index * half : (index + 1) * half] = normed.astype(BF16)

    out_ref[...] = (cand_ref[...].astype(F32) + dot(normed_ref[...], w_ref[...])).astype(BF16)


def tail(got, place, gates, terms, candidates, w_out):
    rows, width = candidates.shape
    half = width // 2
    block = min(256, width)

    def fixed(array):
        zeros = (0,) * array.ndim
        return pl.BlockSpec(array.shape, lambda j: zeros)

    return pl.pallas_call(
        tail_kernel,
        grid=(width // block,),
        in_specs=[
            fixed(got),
            fixed(place),
            fixed(gates[0]),
            fixed(gates[1]),
            fixed(terms[0]),
            fixed(terms[1]),
            pl.BlockSpec((rows, block), lambda j: (0, j)),
            pl.BlockSpec((width, block), lambda j: (0, j)),
        ],
        out_specs=pl.BlockSpec((rows, block), lambda j: (0, j)),
        out_shape=jax.ShapeDtypeStruct((rows, width), BF16),
        scratch_shapes=[pltpu.VMEM((rows, width), BF16)],
        compiler_params=pltpu.CompilerParams(vmem_limit_bytes=40 << 20),
        cost_estimate=pl.CostEstimate(
            flops=2 * rows * width * (width + got.shape[0] * 8), bytes_accessed=6 << 20, transcendentals=rows
        ),
        name="tail",
    )(got, place, *gates, *terms, candidates, w_out)


def exchange(rows):
    tiles, pair, eight, half = rows.shape
    flat = rows.reshape(tiles * pair, eight, half)
    return lax.all_to_all(flat, "serve", split_axis=0, concat_axis=0, tiled=True).reshape(rows.shape)


def per_device(history, candidates, cand_user, hist_len, w_uvqk, w_out):
    users = lax.axis_size("serve")
    outgoing, query0, query1, place = front(cand_user, candidates, w_uvqk, users)
    other = lax.ppermute(history, "rep", [(0, 1), (1, 0)])
    outgoing, history, query0, query1 = lax.optimization_barrier((outgoing, history, query0, query1))
    received = exchange(outgoing)
    info = jnp.concatenate([hist_len, lax.axis_index("rep").astype(jnp.int32)[None]])
    kv = keys_vals(info, history, other, w_uvqk)
    pairs = [own_part(candidates, query, w_uvqk, index) for index, query in enumerate((query0, query1))]
    gates, terms = [pair[0] for pair in pairs], [pair[1] for pair in pairs]
    returned = exchange(attention(received, kv))
    return tail(returned, place, gates, terms, candidates, w_out)


def solution(mesh):
    placed = (
        P(("serve", "rep"), None),
        P(("serve", "rep"), None),
        P(("serve", "rep"), None),
        P("serve"),
        P(),
        P(),
    )
    return jax.shard_map(
        per_device, mesh=mesh, in_specs=placed, out_specs=P(("serve", "rep"), None), check_vma=False
    )
```

```python
import functools
import math

import jax
import jax.numpy as jnp
from jax import lax
from jax.experimental import pallas as pl
from jax.experimental.pallas import tpu as pltpu
from jax.sharding import PartitionSpec as P

HEADS = 8
CAP = 4
FRONT_PARTS = 4
FRONT_OUTS = 2
VMEM_LIMIT = 60 << 20
BF16 = jnp.bfloat16
F32 = jnp.float32


def silu(x):
    y = 0.5 * x
    return y + y * jnp.tanh(y)


def dot(a, b):
    return jnp.dot(a, b, preferred_element_type=F32)


def weave(first, second):
    low = lax.broadcasted_iota(jnp.int32, first.shape, 1) < 4
    even = jnp.where(low, first, pltpu.roll(second, 4, 1))
    odd = jnp.where(low, pltpu.roll(first, 4, 1), second)
    return even, odd


def params():
    return pltpu.CompilerParams(vmem_limit_bytes=VMEM_LIMIT)


def front_kernel(user_ref, cand_hbm, w_hbm, out_hbm, query_ref, place_ref, cand_ref, w_ref, out_ref, in_sems, out_sems):
    slots, rows = place_ref.shape
    users = slots // CAP
    width = cand_ref.shape[1]
    half = width // 2
    parts = w_ref.shape[0]
    depth = width // parts
    copies = [pltpu.make_async_copy(cand_hbm, cand_ref, in_sems.at[parts])]
    for index in range(parts):
        source = w_hbm.at[pl.ds(index * depth, depth), pl.ds(2 * width, width)]
        copies.append(pltpu.make_async_copy(source, w_ref.at[index], in_sems.at[index]))
    for copy in copies:
        copy.start()

    ids = user_ref[...]
    one_hot = jnp.where(ids == lax.broadcasted_iota(jnp.int32, (users, rows), 0), 1.0, 0.0)
    earlier = jnp.where(
        lax.broadcasted_iota(jnp.int32, (rows, rows), 0)
        < lax.broadcasted_iota(jnp.int32, (rows, rows), 1),
        1.0,
        0.0,
    )
    before = dot(one_hot.astype(BF16), earlier.astype(BF16))
    rank = jnp.sum(before * one_hot, 0, keepdims=True).astype(jnp.int32)
    slot = ids * CAP + rank
    place = jnp.where(slot == lax.broadcasted_iota(jnp.int32, (slots, rows), 0), 1.0, 0.0).astype(BF16)
    place_ref[...] = place

    copies[0].wait()
    total = None
    for index in range(parts):
        copies[1 + index].wait()
        term = dot(cand_ref[:, index * depth : (index + 1) * depth], w_ref[index])
        total = term if total is None else total + term
    query = silu(total).astype(BF16)
    query_ref[...] = query
    block = half // out_sems.shape[0]
    outs = []
    for index in range(half // block):
        pair = []
        for start in (index * block, half + index * block):
            moved = dot(place, query[:, start : start + block])
            pair.append(moved.reshape(slots // 8, 8, block))
        even, odd = weave(*pair)
        columns = pl.ds(index * block, block)
        out_ref[:, 0, :, columns] = even.astype(BF16)
        out_ref[:, 1, :, columns] = odd.astype(BF16)
        copy = pltpu.make_async_copy(
            out_ref.at[:, :, :, columns], out_hbm.at[:, :, :, columns], out_sems.at[index]
        )
        copy.start()
        outs.append(copy)
    for copy in outs:
        copy.wait()


def front(cand_user, candidates, w_uvqk, users):
    rows, width = candidates.shape
    half = width // 2
    slots = users * CAP
    parts = FRONT_PARTS
    whole = pl.BlockSpec(memory_space=pl.ANY)
    inside = pl.BlockSpec(memory_space=pltpu.VMEM)
    tiles = (slots // 8, 2, 8, half)
    return pl.pallas_call(
        front_kernel,
        in_specs=[inside, whole, whole],
        out_specs=[whole, inside, inside],
        out_shape=[
            jax.ShapeDtypeStruct(tiles, BF16),
            jax.ShapeDtypeStruct((rows, width), BF16),
            jax.ShapeDtypeStruct((slots, rows), BF16),
        ],
        scratch_shapes=[
            pltpu.VMEM((rows, width), BF16),
            pltpu.VMEM((parts, width // parts, width), BF16),
            pltpu.VMEM(tiles, BF16),
            pltpu.SemaphoreType.DMA((parts + 1,)),
            pltpu.SemaphoreType.DMA((FRONT_OUTS,)),
        ],
        compiler_params=params(),
        cost_estimate=pl.CostEstimate(
            flops=2 * rows * width * (width + slots), bytes_accessed=5 << 20, transcendentals=rows * width
        ),
        name="front",
    )(cand_user.reshape(1, rows), candidates, w_uvqk)


def keys_vals_kernel(steps, info_ref, own_ref, other_ref, w_ref, key_ref, value_ref):
    count = own_ref.shape[0]
    weight = w_ref[...]
    for part, ref in enumerate((own_ref, other_ref)):
        result = silu(dot(ref[...], weight))
        span = slice(part * count, (part + 1) * count)

        @pl.when(pl.program_id(0) < steps)
        def _():
            key_ref[:, span] = result.T.astype(BF16)

        @pl.when(pl.program_id(0) >= steps)
        def _():
            start = jnp.where(info_ref[1] == part, 0, count)
            event = start + lax.broadcasted_iota(jnp.int32, result.shape, 0)
            value = jnp.where(event < info_ref[0], result, 0.0).astype(BF16)
            head_size = value_ref.shape[2]
            for head in range(value_ref.shape[0]):
                value_ref[head, span] = value[:, head * head_size : (head + 1) * head_size]


def keys_vals(info, own, other, w_uvqk):
    count, width = own.shape
    block = min(256, width)
    steps = width // block
    return pl.pallas_call(
        functools.partial(keys_vals_kernel, steps),
        grid=(2 * steps,),
        in_specs=[
            pl.BlockSpec(memory_space=pltpu.SMEM),
            pl.BlockSpec((count, width), lambda j: (0, 0)),
            pl.BlockSpec((count, width), lambda j: (0, 0)),
            pl.BlockSpec((width, block), lambda j: (0, jnp.where(j < steps, 3 * steps + j, j))),
        ],
        out_specs=[
            pl.BlockSpec((block, 2 * count), lambda j: (jnp.minimum(j, steps - 1), 0)),
            pl.BlockSpec((HEADS // steps, 2 * count, width // HEADS), lambda j: (jnp.maximum(j - steps, 0), 0, 0)),
        ],
        out_shape=[
            jax.ShapeDtypeStruct((width, 2 * count), BF16),
            jax.ShapeDtypeStruct((HEADS, 2 * count, width // HEADS), BF16),
        ],
        compiler_params=params(),
        cost_estimate=pl.CostEstimate(
            flops=8 * count * width * width, bytes_accessed=10 << 20, transcendentals=4 * count * width
        ),
        name="keys_vals",
    )(info, own, other, w_uvqk)


def attention_kernel(got_hbm, key_hbm, value_hbm, out_hbm, got_ref, key_ref, value_ref, out_ref, in_sems, out_sems):
    tiles, _, _, half = got_ref.shape
    slots = tiles * 8
    head_size = 2 * half // HEADS
    pairs = HEADS // 2
    got_copy = pltpu.make_async_copy(got_hbm, got_ref, in_sems.at[2 * HEADS])
    got_copy.start()
    copies = {}
    for pair in range(pairs):
        for head in (pair, pairs + pair):
            rows = pl.ds(head * head_size, head_size)
            copies[head] = (
                pltpu.make_async_copy(key_hbm.at[rows], key_ref.at[head], in_sems.at[head]),
                pltpu.make_async_copy(value_hbm.at[head], value_ref.at[head], in_sems.at[HEADS + head]),
            )
            for copy in copies[head]:
                copy.start()
    scale = 0.5 / math.sqrt(head_size)
    got_copy.wait()
    outs = []
    for pair in range(pairs):
        columns = pl.ds(pair * head_size, head_size)
        for head in (pair, pairs + pair):
            for copy in copies[head]:
                copy.wait()
        queries = weave(got_ref[:, 0, :, columns].astype(F32), got_ref[:, 1, :, columns].astype(F32))
        results = []
        for query, head in zip(queries, (pair, pairs + pair)):
            rows = query.reshape(slots, head_size).astype(BF16)
            y = dot(rows, key_ref[head]) * scale
            weights = (y + y * jnp.tanh(y)).astype(BF16)
            results.append(dot(weights, value_ref[head]).reshape(tiles, 8, head_size))
        even, odd = weave(*results)
        out_ref[:, 0, :, columns] = even.astype(BF16)
        out_ref[:, 1, :, columns] = odd.astype(BF16)
        copy = pltpu.make_async_copy(
            out_ref.at[:, :, :, columns], out_hbm.at[:, :, :, columns], out_sems.at[pair]
        )
        copy.start()
        outs.append(copy)
    for copy in outs:
        copy.wait()


def attention(got, keys, values):
    tiles, _, _, half = got.shape
    slots = tiles * 8
    heads, events, head_size = values.shape
    whole = pl.BlockSpec(memory_space=pl.ANY)
    return pl.pallas_call(
        attention_kernel,
        in_specs=[whole] * 3,
        out_specs=whole,
        out_shape=jax.ShapeDtypeStruct(got.shape, BF16),
        scratch_shapes=[
            pltpu.VMEM(got.shape, BF16),
            pltpu.VMEM((heads, head_size, events), BF16),
            pltpu.VMEM((heads, events, head_size), BF16),
            pltpu.VMEM(got.shape, BF16),
            pltpu.SemaphoreType.DMA((2 * heads + 1,)),
            pltpu.SemaphoreType.DMA((heads // 2,)),
        ],
        compiler_params=params(),
        cost_estimate=pl.CostEstimate(
            flops=8 * slots * events * half,
            bytes_accessed=6 << 20,
            transcendentals=slots * events * heads,
        ),
        name="attention",
    )(got, keys, values)


def own_kernel(head_size, cand_ref, query_ref, wg_ref, wv_ref, wk_ref, place_ref, gate_ref, term_ref, turned_ref):
    @pl.when(pl.program_id(0) == 0)
    def _():
        turned_ref[...] = place_ref[...].astype(F32).T.astype(BF16)

    cand = cand_ref[...]
    gate_ref[...] = silu(dot(cand, wg_ref[...])).astype(BF16)
    value = silu(dot(cand, wv_ref[...])).astype(BF16).astype(F32)
    key = silu(dot(cand, wk_ref[...])).astype(BF16).astype(F32)
    product = query_ref[...].astype(F32) * key
    for start in range(0, product.shape[1], head_size):
        columns = slice(start, start + head_size)
        score = jnp.sum(product[:, columns], 1, keepdims=True) / math.sqrt(head_size)
        term_ref[:, columns] = silu(score) * value[:, columns]


def own_part(candidates, query, w_uvqk, place):
    rows, width = candidates.shape
    slots = place.shape[0]
    block = 256
    steps = width // block
    column = pl.BlockSpec((rows, block), lambda j: (0, j))
    return pl.pallas_call(
        functools.partial(own_kernel, width // HEADS),
        grid=(steps,),
        in_specs=[
            pl.BlockSpec((rows, width), lambda j: (0, 0)),
            column,
            pl.BlockSpec((width, block), lambda j: (0, j)),
            pl.BlockSpec((width, block), lambda j: (0, steps + j)),
            pl.BlockSpec((width, block), lambda j: (0, 3 * steps + j)),
            pl.BlockSpec((slots, rows), lambda j: (0, 0)),
        ],
        out_specs=[column, column, pl.BlockSpec((rows, slots), lambda j: (0, 0))],
        out_shape=[
            jax.ShapeDtypeStruct((rows, width), BF16),
            jax.ShapeDtypeStruct((rows, width), F32),
            jax.ShapeDtypeStruct((rows, slots), BF16),
        ],
        compiler_params=params(),
        cost_estimate=pl.CostEstimate(
            flops=6 * rows * width * width, bytes_accessed=9 << 20, transcendentals=3 * rows * width
        ),
        name="own_part",
    )(candidates, query, w_uvqk, w_uvqk, w_uvqk, place)


def tail_kernel(*refs):
    sources, out_hbm = refs[:6], refs[6]
    buffers, out_ref = refs[7:13], refs[13]
    in_sems, out_sems = refs[14], refs[15]
    copies = [
        pltpu.make_async_copy(source, buffer, in_sems.at[index])
        for index, (source, buffer) in enumerate(zip(sources, buffers))
    ]
    for copy in copies:
        copy.start()
    place_ref, got_ref, term_ref, gate_ref, w_ref, cand_ref = buffers
    tiles, _, _, half = got_ref.shape
    width = 2 * half
    copies[0].wait()
    copies[1].wait()
    place = place_ref[...]
    parts = weave(got_ref[:, 0].astype(F32), got_ref[:, 1].astype(F32))
    history = [dot(place, part.reshape(tiles * 8, half).astype(BF16)) for part in parts]
    copies[2].wait()
    attended = jnp.concatenate(history, 1) + term_ref[...]
    mean = jnp.sum(attended, 1, keepdims=True) / width
    centred = attended - mean
    var = jnp.sum(centred * centred, 1, keepdims=True) / width
    scaled = centred * lax.rsqrt(var + 1e-05)
    copies[3].wait()
    normed = (scaled * gate_ref[...].astype(F32)).astype(BF16)
    copies[4].wait()
    copies[5].wait()
    block = 256
    outs = []
    for index in range(width // block):
        columns = slice(index * block, (index + 1) * block)
        result = cand_ref[:, columns].astype(F32) + dot(normed, w_ref[:, columns])
        out_ref[:, columns] = result.astype(BF16)
        copy = pltpu.make_async_copy(
            out_ref.at[:, pl.ds(index * block, block)],
            out_hbm.at[:, pl.ds(index * block, block)],
            out_sems.at[index],
        )
        copy.start()
        outs.append(copy)
    for copy in outs:
        copy.wait()


def tail(got, place, gate, term, candidates, w_out):
    rows, width = candidates.shape
    sources = (place, got, term, gate, w_out, candidates)
    return pl.pallas_call(
        tail_kernel,
        in_specs=[pl.BlockSpec(memory_space=pl.ANY)] * 6,
        out_specs=pl.BlockSpec(memory_space=pl.ANY),
        out_shape=jax.ShapeDtypeStruct((rows, width), BF16),
        scratch_shapes=[pltpu.VMEM(source.shape, source.dtype) for source in sources]
        + [
            pltpu.VMEM((rows, width), BF16),
            pltpu.SemaphoreType.DMA((6,)),
            pltpu.SemaphoreType.DMA((width // 256,)),
        ],
        compiler_params=params(),
        cost_estimate=pl.CostEstimate(
            flops=2 * rows * width * (width + got.shape[0] * 8), bytes_accessed=6 << 20, transcendentals=rows
        ),
        name="tail",
    )(*sources)


def exchange(rows):
    tiles, pair, eight, half = rows.shape
    flat = rows.reshape(tiles * pair, eight, half)
    return lax.all_to_all(flat, "serve", split_axis=0, concat_axis=0, tiled=True).reshape(rows.shape)


def per_device(history, candidates, cand_user, hist_len, w_uvqk, w_out):
    users = lax.axis_size("serve")
    outgoing, query, place = front(cand_user, candidates, w_uvqk, users)
    other = lax.ppermute(history, "rep", [(0, 1), (1, 0)])
    outgoing, history, query = lax.optimization_barrier((outgoing, history, query))
    received = exchange(outgoing)
    info = jnp.concatenate([hist_len, lax.axis_index("rep").astype(jnp.int32)[None]])
    keys, values = keys_vals(info, history, other, w_uvqk)
    gate, term, turned = own_part(candidates, query, w_uvqk, place)
    returned = exchange(attention(received, keys, values))
    return tail(returned, turned, gate, term, candidates, w_out)


def solution(mesh):
    placed = (
        P(("serve", "rep"), None),
        P(("serve", "rep"), None),
        P(("serve", "rep"), None),
        P("serve"),
        P(),
        P(),
    )
    return jax.shard_map(
        per_device, mesh=mesh, in_specs=placed, out_specs=P(("serve", "rep"), None), check_vma=False
    )
```

```python
import functools
import math

import jax
import jax.numpy as jnp
from jax import lax
from jax.experimental import pallas as pl
from jax.experimental.pallas import tpu as pltpu
from jax.sharding import PartitionSpec as P

HEADS = 8
CAP = 4
BF16 = jnp.bfloat16
F32 = jnp.float32


def silu(x):
    y = 0.5 * x
    return y + y * jnp.tanh(y)


def dot(a, b):
    return jnp.dot(a, b, preferred_element_type=F32)


def turn(matrix, identity):
    turned = lax.dot_general(matrix, identity, (((0,), (0,)), ((), ())), preferred_element_type=F32)
    return turned.astype(BF16)


def weave(first, second):
    low = lax.broadcasted_iota(jnp.int32, first.shape, 1) < 4
    even = jnp.where(low, first, pltpu.roll(second, 4, 1))
    odd = jnp.where(low, pltpu.roll(first, 4, 1), second)
    return even, odd


def params(limit=60):
    return pltpu.CompilerParams(vmem_limit_bytes=limit << 20)


def front_kernel(
    user_hbm, cand_hbm, w_hbm, out_hbm, place_hbm, user_ref, cand_ref, w_ref, out_ref, place_ref, in_sems, out_sems
):
    slots, rows = place_ref.shape
    users = slots // CAP
    width = cand_ref.shape[1]
    parts, _, block = w_ref.shape
    steps = parts // 2
    copies = [
        pltpu.make_async_copy(user_hbm, user_ref, in_sems.at[0]),
        pltpu.make_async_copy(cand_hbm, cand_ref, in_sems.at[1]),
    ]
    for index in range(steps):
        for part in (index, steps + index):
            source = w_hbm.at[:, pl.ds(2 * width + part * block, block)]
            copies.append(pltpu.make_async_copy(source, w_ref.at[part], in_sems.at[2 + part]))
    for copy in copies:
        copy.start()

    copies[0].wait()
    ids = user_ref[...]
    one_hot = jnp.where(ids == lax.broadcasted_iota(jnp.int32, (users, rows), 0), 1.0, 0.0)
    earlier = jnp.where(
        lax.broadcasted_iota(jnp.int32, (rows, rows), 0)
        < lax.broadcasted_iota(jnp.int32, (rows, rows), 1),
        1.0,
        0.0,
    )
    before = dot(one_hot.astype(BF16), earlier.astype(BF16))
    rank = jnp.sum(before * one_hot, 0, keepdims=True).astype(jnp.int32)
    slot = ids * CAP + rank
    place = jnp.where(slot == lax.broadcasted_iota(jnp.int32, (slots, rows), 0), 1.0, 0.0).astype(BF16)
    place_ref[...] = place
    outs = [pltpu.make_async_copy(place_ref, place_hbm, out_sems.at[0])]
    outs[0].start()

    copies[1].wait()
    for index in range(steps):
        pair = []
        for offset, part in enumerate((index, steps + index)):
            copies[2 + 2 * index + offset].wait()
            query = silu(dot(cand_ref[...], w_ref[part])).astype(BF16)
            pair.append(dot(place, query).reshape(slots // 8, 8, block))
        even, odd = weave(*pair)
        columns = pl.ds(index * block, block)
        out_ref[:, 0, :, columns] = even.astype(BF16)
        out_ref[:, 1, :, columns] = odd.astype(BF16)
        copy = pltpu.make_async_copy(
            out_ref.at[:, :, :, columns], out_hbm.at[:, :, :, columns], out_sems.at[1 + index]
        )
        copy.start()
        outs.append(copy)
    for copy in outs:
        copy.wait()


def front(cand_user, candidates, w_uvqk, users):
    rows, width = candidates.shape
    half = width // 2
    slots = users * CAP
    block = 256
    parts = width // block
    whole = pl.BlockSpec(memory_space=pl.ANY)
    tiles = (slots // 8, 2, 8, half)
    return pl.pallas_call(
        front_kernel,
        in_specs=[whole] * 3,
        out_specs=[whole] * 2,
        out_shape=[
            jax.ShapeDtypeStruct(tiles, BF16),
            jax.ShapeDtypeStruct((slots, rows), BF16),
        ],
        scratch_shapes=[
            pltpu.VMEM((1, rows), jnp.int32),
            pltpu.VMEM((rows, width), BF16),
            pltpu.VMEM((parts, width, block), BF16),
            pltpu.VMEM(tiles, BF16),
            pltpu.VMEM((slots, rows), BF16),
            pltpu.SemaphoreType.DMA((parts + 2,)),
            pltpu.SemaphoreType.DMA((parts // 2 + 1,)),
        ],
        compiler_params=params(),
        cost_estimate=pl.CostEstimate(
            flops=2 * rows * width * (width + slots), bytes_accessed=5 << 20, transcendentals=rows * width
        ),
        name="front",
    )(cand_user.reshape(1, rows), candidates, w_uvqk)


def keys_vals_kernel(steps, info_ref, own_ref, other_ref, w_ref, key_ref, value_ref):
    count = own_ref.shape[0]
    weight = w_ref[...]
    for part, ref in enumerate((own_ref, other_ref)):
        result = silu(dot(ref[...], weight))
        span = slice(part * count, (part + 1) * count)

        @pl.when(pl.program_id(0) < steps)
        def _():
            row = lax.broadcasted_iota(jnp.int32, (count, count), 0)
            column = lax.broadcasted_iota(jnp.int32, (count, count), 1)
            identity = jnp.where(row == column, 1.0, 0.0).astype(BF16)
            key_ref[:, span] = turn(result.astype(BF16), identity)

        @pl.when(pl.program_id(0) >= steps)
        def _():
            start = jnp.where(info_ref[1] == part, 0, count)
            event = start + lax.broadcasted_iota(jnp.int32, result.shape, 0)
            value = jnp.where(event < info_ref[0], result, 0.0).astype(BF16)
            head_size = value_ref.shape[2]
            for head in range(value_ref.shape[0]):
                value_ref[head, span] = value[:, head * head_size : (head + 1) * head_size]


def keys_vals(info, own, other, w_uvqk):
    count, width = own.shape
    block = min(256, width)
    steps = width // block
    return pl.pallas_call(
        functools.partial(keys_vals_kernel, steps),
        grid=(2 * steps,),
        in_specs=[
            pl.BlockSpec(memory_space=pltpu.SMEM),
            pl.BlockSpec((count, width), lambda j: (0, 0)),
            pl.BlockSpec((count, width), lambda j: (0, 0)),
            pl.BlockSpec((width, block), lambda j: (0, jnp.where(j < steps, 3 * steps + j, j))),
        ],
        out_specs=[
            pl.BlockSpec((block, 2 * count), lambda j: (jnp.minimum(j, steps - 1), 0)),
            pl.BlockSpec((HEADS // steps, 2 * count, width // HEADS), lambda j: (jnp.maximum(j - steps, 0), 0, 0)),
        ],
        out_shape=[
            jax.ShapeDtypeStruct((width, 2 * count), BF16),
            jax.ShapeDtypeStruct((HEADS, 2 * count, width // HEADS), BF16),
        ],
        compiler_params=params(),
        cost_estimate=pl.CostEstimate(
            flops=8 * count * width * width, bytes_accessed=10 << 20, transcendentals=4 * count * width
        ),
        name="keys_vals",
    )(info, own, other, w_uvqk)


def attention_kernel(got_hbm, key_hbm, value_hbm, out_hbm, got_ref, key_ref, value_ref, out_ref, in_sems, out_sems):
    tiles, _, _, half = got_ref.shape
    slots = tiles * 8
    head_size = 2 * half // HEADS
    pairs = HEADS // 2
    got_copy = pltpu.make_async_copy(got_hbm, got_ref, in_sems.at[2 * HEADS])
    got_copy.start()
    copies = {}
    for pair in range(pairs):
        for head in (pair, pairs + pair):
            rows = pl.ds(head * head_size, head_size)
            copies[head] = (
                pltpu.make_async_copy(key_hbm.at[rows], key_ref.at[head], in_sems.at[head]),
                pltpu.make_async_copy(value_hbm.at[head], value_ref.at[head], in_sems.at[HEADS + head]),
            )
            for copy in copies[head]:
                copy.start()
    scale = 0.5 / math.sqrt(head_size)
    got_copy.wait()
    outs = []
    for pair in range(pairs):
        columns = pl.ds(pair * head_size, head_size)
        for head in (pair, pairs + pair):
            for copy in copies[head]:
                copy.wait()
        queries = weave(got_ref[:, 0, :, columns].astype(F32), got_ref[:, 1, :, columns].astype(F32))
        results = []
        for query, head in zip(queries, (pair, pairs + pair)):
            rows = query.reshape(slots, head_size).astype(BF16)
            y = dot(rows, key_ref[head]) * scale
            weights = (y + y * jnp.tanh(y)).astype(BF16)
            results.append(dot(weights, value_ref[head]).reshape(tiles, 8, head_size))
        even, odd = weave(*results)
        out_ref[:, 0, :, columns] = even.astype(BF16)
        out_ref[:, 1, :, columns] = odd.astype(BF16)
        copy = pltpu.make_async_copy(
            out_ref.at[:, :, :, columns], out_hbm.at[:, :, :, columns], out_sems.at[pair]
        )
        copy.start()
        outs.append(copy)
    for copy in outs:
        copy.wait()


def attention(got, keys, values):
    tiles, _, _, half = got.shape
    slots = tiles * 8
    heads, events, head_size = values.shape
    whole = pl.BlockSpec(memory_space=pl.ANY)
    return pl.pallas_call(
        attention_kernel,
        in_specs=[whole] * 3,
        out_specs=whole,
        out_shape=jax.ShapeDtypeStruct(got.shape, BF16),
        scratch_shapes=[
            pltpu.VMEM(got.shape, BF16),
            pltpu.VMEM((heads, head_size, events), BF16),
            pltpu.VMEM((heads, events, head_size), BF16),
            pltpu.VMEM(got.shape, BF16),
            pltpu.SemaphoreType.DMA((2 * heads + 1,)),
            pltpu.SemaphoreType.DMA((heads // 2,)),
        ],
        compiler_params=params(50),
        cost_estimate=pl.CostEstimate(
            flops=8 * slots * events * half,
            bytes_accessed=6 << 20,
            transcendentals=slots * events * heads,
        ),
        name="attention",
    )(got, keys, values)


def own_kernel(head_size, cand_ref, wg_ref, wv_ref, wq_ref, wk_ref, place_ref, out_ref):
    step = pl.program_id(0)
    block = wg_ref.shape[1]
    rows, width = cand_ref.shape
    slots = place_ref.shape[0]

    @pl.when(step == 0)
    def _():
        out_ref[:, 3 * width : 3 * width + slots] = place_ref[...].astype(F32).T.astype(BF16)

    cand = cand_ref[...]
    gate, value, query, key = (
        silu(dot(cand, ref[...])).astype(BF16) for ref in (wg_ref, wv_ref, wq_ref, wk_ref)
    )
    product = query.astype(F32) * key.astype(F32)
    value = value.astype(F32)
    terms = []
    for start in range(0, block, head_size):
        columns = slice(start, start + head_size)
        score = jnp.sum(product[:, columns], 1, keepdims=True) / math.sqrt(head_size)
        terms.append(silu(score) * value[:, columns])
    term = jnp.concatenate(terms, 1)
    high = term.astype(BF16)
    low = (term - high.astype(F32)).astype(BF16)
    for index, array in enumerate((high, low, gate)):
        start = pl.multiple_of(index * width + step * block, block)
        out_ref[:, pl.ds(start, block)] = array


def own_part(candidates, w_uvqk, place):
    rows, width = candidates.shape
    slots = place.shape[0]
    block = 256
    steps = width // block
    return pl.pallas_call(
        functools.partial(own_kernel, width // HEADS),
        grid=(steps,),
        in_specs=[
            pl.BlockSpec((rows, width), lambda j: (0, 0)),
            pl.BlockSpec((width, block), lambda j: (0, j)),
            pl.BlockSpec((width, block), lambda j: (0, steps + j)),
            pl.BlockSpec((width, block), lambda j: (0, 2 * steps + j)),
            pl.BlockSpec((width, block), lambda j: (0, 3 * steps + j)),
            pl.BlockSpec((slots, rows), lambda j: (0, 0)),
        ],
        out_specs=pl.BlockSpec((rows, 3 * width + slots), lambda j: (0, 0)),
        out_shape=jax.ShapeDtypeStruct((rows, 3 * width + slots), BF16),
        compiler_params=params(),
        cost_estimate=pl.CostEstimate(
            flops=8 * rows * width * width, bytes_accessed=11 << 20, transcendentals=4 * rows * width
        ),
        name="own_part",
    )(candidates, w_uvqk, w_uvqk, w_uvqk, w_uvqk, place)


def tail_kernel(
    got_hbm, own_hbm, cand_hbm, w_hbm, out_hbm, got_ref, own_ref, cand_ref, w_ref, out_ref, in_sems, out_sems
):
    tiles, _, _, half = got_ref.shape
    width = 2 * half
    slots = tiles * 8
    spans = (pl.ds(3 * width, slots), pl.ds(0, 2 * width), pl.ds(2 * width, width))
    got_copy = pltpu.make_async_copy(got_hbm, got_ref, in_sems.at[0])
    place_copy, term_copy, gate_copy = (
        pltpu.make_async_copy(own_hbm.at[:, span], own_ref.at[:, span], in_sems.at[1 + index])
        for index, span in enumerate(spans)
    )
    w_copy = pltpu.make_async_copy(w_hbm, w_ref, in_sems.at[4])
    cand_copy = pltpu.make_async_copy(cand_hbm, cand_ref, in_sems.at[5])
    for copy in (got_copy, place_copy, term_copy, gate_copy, w_copy, cand_copy):
        copy.start()
    got_copy.wait()
    place_copy.wait()
    place = own_ref[:, 3 * width : 3 * width + slots]
    parts = weave(got_ref[:, 0].astype(F32), got_ref[:, 1].astype(F32))
    history = [dot(place, part.reshape(slots, half).astype(BF16)) for part in parts]
    term_copy.wait()
    term = own_ref[:, :width].astype(F32) + own_ref[:, width : 2 * width].astype(F32)
    attended = jnp.concatenate(history, 1) + term
    mean = jnp.sum(attended, 1, keepdims=True) / width
    centred = attended - mean
    var = jnp.sum(centred * centred, 1, keepdims=True) / width
    scaled = centred * lax.rsqrt(var + 1e-05)
    gate_copy.wait()
    normed = (scaled * own_ref[:, 2 * width : 3 * width].astype(F32)).astype(BF16)
    w_copy.wait()
    cand_copy.wait()
    block = 256
    outs = []
    for index in range(width // block):
        columns = slice(index * block, (index + 1) * block)
        result = cand_ref[:, columns].astype(F32) + dot(normed, w_ref[:, columns])
        out_ref[:, columns] = result.astype(BF16)
        span = pl.ds(index * block, block)
        copy = pltpu.make_async_copy(out_ref.at[:, span], out_hbm.at[:, span], out_sems.at[index])
        copy.start()
        outs.append(copy)
    for copy in outs:
        copy.wait()


def tail(got, own, candidates, w_out):
    rows, width = candidates.shape
    sources = (got, own, candidates, w_out)
    return pl.pallas_call(
        tail_kernel,
        in_specs=[pl.BlockSpec(memory_space=pl.ANY)] * 4,
        out_specs=pl.BlockSpec(memory_space=pl.ANY),
        out_shape=jax.ShapeDtypeStruct((rows, width), BF16),
        scratch_shapes=[pltpu.VMEM(source.shape, source.dtype) for source in sources]
        + [
            pltpu.VMEM((rows, width), BF16),
            pltpu.SemaphoreType.DMA((6,)),
            pltpu.SemaphoreType.DMA((width // 256,)),
        ],
        compiler_params=params(51),
        cost_estimate=pl.CostEstimate(
            flops=2 * rows * width * (width + got.shape[0] * 8), bytes_accessed=6 << 20, transcendentals=rows
        ),
        name="tail",
    )(*sources)


def exchange(rows):
    tiles, pair, eight, half = rows.shape
    flat = rows.reshape(tiles * pair, eight, half)
    return lax.all_to_all(flat, "serve", split_axis=0, concat_axis=0, tiled=True).reshape(rows.shape)


def per_device(history, candidates, cand_user, hist_len, w_uvqk, w_out):
    users = lax.axis_size("serve")
    outgoing, place = front(cand_user, candidates, w_uvqk, users)
    other = lax.ppermute(history, "rep", [(0, 1), (1, 0)])
    outgoing, history, place = lax.optimization_barrier((outgoing, history, place))
    received = exchange(outgoing)
    info = jnp.concatenate([hist_len, lax.axis_index("rep").astype(jnp.int32)[None]])
    keys, values = keys_vals(info, history, other, w_uvqk)
    own = own_part(candidates, w_uvqk, place)
    returned = exchange(attention(received, keys, values))
    return tail(returned, own, candidates, w_out)


def solution(mesh):
    placed = (
        P(("serve", "rep"), None),
        P(("serve", "rep"), None),
        P(("serve", "rep"), None),
        P("serve"),
        P(),
        P(),
    )
    return jax.shard_map(
        per_device, mesh=mesh, in_specs=placed, out_specs=P(("serve", "rep"), None), check_vma=False
    )
```

```python
import functools
import math

import jax
import jax.numpy as jnp
from jax import lax
from jax.experimental import pallas as pl
from jax.experimental.pallas import tpu as pltpu
from jax.sharding import PartitionSpec as P

HEADS = 8
CAP = 4
BF16 = jnp.bfloat16
F32 = jnp.float32


def silu(x):
    y = 0.5 * x
    return y + y * jnp.tanh(y)


def dot(a, b):
    return jnp.dot(a, b, preferred_element_type=F32)


def turn(matrix, identity):
    turned = lax.dot_general(matrix, identity, (((0,), (0,)), ((), ())), preferred_element_type=F32)
    return turned.astype(BF16)


def weave(first, second):
    low = lax.broadcasted_iota(jnp.int32, first.shape, 1) < 4
    even = jnp.where(low, first, pltpu.roll(second, 4, 1))
    odd = jnp.where(low, pltpu.roll(first, 4, 1), second)
    return even, odd


def params(limit=60):
    return pltpu.CompilerParams(vmem_limit_bytes=limit << 20)


def front_kernel(
    user_hbm, cand_hbm, w_hbm, out_hbm, place_hbm, user_ref, cand_ref, w_ref, out_ref, place_ref, in_sems, out_sems
):
    slots, rows = place_ref.shape
    users = slots // CAP
    width = cand_ref.shape[1]
    parts, depth, _ = w_ref.shape
    copies = [
        pltpu.make_async_copy(user_hbm, user_ref, in_sems.at[0]),
        pltpu.make_async_copy(cand_hbm, cand_ref, in_sems.at[1]),
    ]
    for index in range(parts):
        source = w_hbm.at[pl.ds(index * depth, depth), pl.ds(2 * width, width)]
        copies.append(pltpu.make_async_copy(source, w_ref.at[index], in_sems.at[2 + index]))
    for copy in copies:
        copy.start()

    copies[0].wait()
    ids = user_ref[...]
    one_hot = jnp.where(ids == lax.broadcasted_iota(jnp.int32, (users, rows), 0), 1.0, 0.0)
    earlier = jnp.where(
        lax.broadcasted_iota(jnp.int32, (rows, rows), 0)
        < lax.broadcasted_iota(jnp.int32, (rows, rows), 1),
        1.0,
        0.0,
    )
    before = dot(one_hot.astype(BF16), earlier.astype(BF16))
    rank = jnp.sum(before * one_hot, 0, keepdims=True).astype(jnp.int32)
    slot = ids * CAP + rank
    place = jnp.where(slot == lax.broadcasted_iota(jnp.int32, (slots, rows), 0), 1.0, 0.0).astype(BF16)
    place_ref[...] = place
    outs = [pltpu.make_async_copy(place_ref, place_hbm, out_sems.at[0])]
    outs[0].start()

    copies[1].wait()
    total = None
    for index in range(parts):
        copies[2 + index].wait()
        term = dot(cand_ref[:, index * depth : (index + 1) * depth], w_ref[index])
        total = term if total is None else total + term
    query = silu(total).astype(BF16)
    half = width // 2
    pieces = out_sems.shape[0] - 1
    count = slots // pieces
    tiles = count // 8
    for index in range(pieces):
        moved = dot(place[index * count : (index + 1) * count], query).reshape(tiles, 8, width)
        even, odd = weave(moved[:, :, :half], moved[:, :, half:])
        span = pl.ds(index * tiles, tiles)
        out_ref[span, 0] = even.astype(BF16)
        out_ref[span, 1] = odd.astype(BF16)
        copy = pltpu.make_async_copy(out_ref.at[span], out_hbm.at[span], out_sems.at[1 + index])
        copy.start()
        outs.append(copy)
    for copy in outs:
        copy.wait()


def front(cand_user, candidates, w_uvqk, users):
    rows, width = candidates.shape
    half = width // 2
    slots = users * CAP
    parts = 4
    pieces = 4
    whole = pl.BlockSpec(memory_space=pl.ANY)
    tiles = (slots // 8, 2, 8, half)
    return pl.pallas_call(
        front_kernel,
        in_specs=[whole] * 3,
        out_specs=[whole] * 2,
        out_shape=[
            jax.ShapeDtypeStruct(tiles, BF16),
            jax.ShapeDtypeStruct((slots, rows), BF16),
        ],
        scratch_shapes=[
            pltpu.VMEM((1, rows), jnp.int32),
            pltpu.VMEM((rows, width), BF16),
            pltpu.VMEM((parts, width // parts, width), BF16),
            pltpu.VMEM(tiles, BF16),
            pltpu.VMEM((slots, rows), BF16),
            pltpu.SemaphoreType.DMA((parts + 2,)),
            pltpu.SemaphoreType.DMA((pieces + 1,)),
        ],
        compiler_params=params(),
        cost_estimate=pl.CostEstimate(
            flops=2 * rows * width * (width + slots), bytes_accessed=5 << 20, transcendentals=rows * width
        ),
        name="front",
    )(cand_user.reshape(1, rows), candidates, w_uvqk)


def keys_vals_kernel(steps, info_ref, own_ref, other_ref, w_ref, key_ref, value_ref):
    count = own_ref.shape[0]
    weight = w_ref[...]
    for part, ref in enumerate((own_ref, other_ref)):
        result = silu(dot(ref[...], weight))
        span = slice(part * count, (part + 1) * count)

        @pl.when(pl.program_id(0) < steps)
        def _():
            row = lax.broadcasted_iota(jnp.int32, (count, count), 0)
            column = lax.broadcasted_iota(jnp.int32, (count, count), 1)
            identity = jnp.where(row == column, 1.0, 0.0).astype(BF16)
            key_ref[:, span] = turn(result.astype(BF16), identity)

        @pl.when(pl.program_id(0) >= steps)
        def _():
            start = jnp.where(info_ref[1] == part, 0, count)
            event = start + lax.broadcasted_iota(jnp.int32, result.shape, 0)
            value = jnp.where(event < info_ref[0], result, 0.0).astype(BF16)
            head_size = value_ref.shape[2]
            for head in range(value_ref.shape[0]):
                value_ref[head, span] = value[:, head * head_size : (head + 1) * head_size]


def keys_vals(info, own, other, w_uvqk):
    count, width = own.shape
    block = min(256, width)
    steps = width // block
    return pl.pallas_call(
        functools.partial(keys_vals_kernel, steps),
        grid=(2 * steps,),
        in_specs=[
            pl.BlockSpec(memory_space=pltpu.SMEM),
            pl.BlockSpec((count, width), lambda j: (0, 0)),
            pl.BlockSpec((count, width), lambda j: (0, 0)),
            pl.BlockSpec((width, block), lambda j: (0, jnp.where(j < steps, 3 * steps + j, j))),
        ],
        out_specs=[
            pl.BlockSpec((block, 2 * count), lambda j: (jnp.minimum(j, steps - 1), 0)),
            pl.BlockSpec((HEADS // steps, 2 * count, width // HEADS), lambda j: (jnp.maximum(j - steps, 0), 0, 0)),
        ],
        out_shape=[
            jax.ShapeDtypeStruct((width, 2 * count), BF16),
            jax.ShapeDtypeStruct((HEADS, 2 * count, width // HEADS), BF16),
        ],
        compiler_params=params(),
        cost_estimate=pl.CostEstimate(
            flops=8 * count * width * width, bytes_accessed=10 << 20, transcendentals=4 * count * width
        ),
        name="keys_vals",
    )(info, own, other, w_uvqk)


def attention_kernel(got_hbm, key_hbm, value_hbm, out_hbm, got_ref, key_ref, value_ref, out_ref, in_sems, out_sems):
    tiles, _, _, half = got_ref.shape
    slots = tiles * 8
    head_size = 2 * half // HEADS
    pairs = HEADS // 2
    got_copy = pltpu.make_async_copy(got_hbm, got_ref, in_sems.at[2 * HEADS])
    got_copy.start()
    copies = {}
    for pair in range(pairs):
        for head in (pair, pairs + pair):
            rows = pl.ds(head * head_size, head_size)
            copies[head] = (
                pltpu.make_async_copy(key_hbm.at[rows], key_ref.at[head], in_sems.at[head]),
                pltpu.make_async_copy(value_hbm.at[head], value_ref.at[head], in_sems.at[HEADS + head]),
            )
            for copy in copies[head]:
                copy.start()
    scale = 0.5 / math.sqrt(head_size)
    got_copy.wait()
    for pair in range(pairs):
        columns = pl.ds(pair * head_size, head_size)
        for head in (pair, pairs + pair):
            for copy in copies[head]:
                copy.wait()
        queries = weave(got_ref[:, 0, :, columns].astype(F32), got_ref[:, 1, :, columns].astype(F32))
        results = []
        for query, head in zip(queries, (pair, pairs + pair)):
            rows = query.reshape(slots, head_size).astype(BF16)
            y = dot(rows, key_ref[head]) * scale
            weights = (y + y * jnp.tanh(y)).astype(BF16)
            results.append(dot(weights, value_ref[head]).reshape(tiles, 8, head_size))
        even, odd = weave(*results)
        out_ref[:, 0, :, columns] = even.astype(BF16)
        out_ref[:, 1, :, columns] = odd.astype(BF16)
    copy = pltpu.make_async_copy(out_ref, out_hbm, out_sems.at[0])
    copy.start()
    copy.wait()


def attention(got, keys, values):
    tiles, _, _, half = got.shape
    slots = tiles * 8
    heads, events, head_size = values.shape
    whole = pl.BlockSpec(memory_space=pl.ANY)
    return pl.pallas_call(
        attention_kernel,
        in_specs=[whole] * 3,
        out_specs=whole,
        out_shape=jax.ShapeDtypeStruct(got.shape, BF16),
        scratch_shapes=[
            pltpu.VMEM(got.shape, BF16),
            pltpu.VMEM((heads, head_size, events), BF16),
            pltpu.VMEM((heads, events, head_size), BF16),
            pltpu.VMEM(got.shape, BF16),
            pltpu.SemaphoreType.DMA((2 * heads + 1,)),
            pltpu.SemaphoreType.DMA((heads // 2,)),
        ],
        compiler_params=params(50),
        cost_estimate=pl.CostEstimate(
            flops=8 * slots * events * half,
            bytes_accessed=6 << 20,
            transcendentals=slots * events * heads,
        ),
        name="attention",
    )(got, keys, values)


def own_kernel(head_size, cand_ref, wg_ref, wv_ref, wq_ref, wk_ref, place_ref, out_ref):
    step = pl.program_id(0)
    block = wg_ref.shape[1]
    rows, width = cand_ref.shape
    slots = place_ref.shape[0]

    @pl.when(step == 0)
    def _():
        out_ref[:, 3 * width : 3 * width + slots] = place_ref[...].astype(F32).T.astype(BF16)

    cand = cand_ref[...]
    gate, value, query, key = (
        silu(dot(cand, ref[...])).astype(BF16) for ref in (wg_ref, wv_ref, wq_ref, wk_ref)
    )
    product = query.astype(F32) * key.astype(F32)
    value = value.astype(F32)
    terms = []
    for start in range(0, block, head_size):
        columns = slice(start, start + head_size)
        score = jnp.sum(product[:, columns], 1, keepdims=True) / math.sqrt(head_size)
        terms.append(silu(score) * value[:, columns])
    term = jnp.concatenate(terms, 1)
    high = term.astype(BF16)
    low = (term - high.astype(F32)).astype(BF16)
    for index, array in enumerate((high, low, gate)):
        start = pl.multiple_of(index * width + step * block, block)
        out_ref[:, pl.ds(start, block)] = array


def own_part(candidates, w_uvqk, place):
    rows, width = candidates.shape
    slots = place.shape[0]
    block = 256
    steps = width // block
    return pl.pallas_call(
        functools.partial(own_kernel, width // HEADS),
        grid=(steps,),
        in_specs=[
            pl.BlockSpec((rows, width), lambda j: (0, 0)),
            pl.BlockSpec((width, block), lambda j: (0, j)),
            pl.BlockSpec((width, block), lambda j: (0, steps + j)),
            pl.BlockSpec((width, block), lambda j: (0, 2 * steps + j)),
            pl.BlockSpec((width, block), lambda j: (0, 3 * steps + j)),
            pl.BlockSpec((slots, rows), lambda j: (0, 0)),
        ],
        out_specs=pl.BlockSpec((rows, 3 * width + slots), lambda j: (0, 0)),
        out_shape=jax.ShapeDtypeStruct((rows, 3 * width + slots), BF16),
        compiler_params=params(),
        cost_estimate=pl.CostEstimate(
            flops=8 * rows * width * width, bytes_accessed=11 << 20, transcendentals=4 * rows * width
        ),
        name="own_part",
    )(candidates, w_uvqk, w_uvqk, w_uvqk, w_uvqk, place)


def tail_kernel(
    got_hbm, own_hbm, cand_hbm, w_hbm, out_hbm, got_ref, own_ref, cand_ref, w_ref, out_ref, in_sems, out_sems
):
    tiles, _, _, half = got_ref.shape
    width = 2 * half
    slots = tiles * 8
    spans = (pl.ds(3 * width, slots), pl.ds(0, 2 * width), pl.ds(2 * width, width))
    got_copy = pltpu.make_async_copy(got_hbm, got_ref, in_sems.at[0])
    place_copy, term_copy, gate_copy = (
        pltpu.make_async_copy(own_hbm.at[:, span], own_ref.at[:, span], in_sems.at[1 + index])
        for index, span in enumerate(spans)
    )
    w_copy = pltpu.make_async_copy(w_hbm, w_ref, in_sems.at[4])
    cand_copy = pltpu.make_async_copy(cand_hbm, cand_ref, in_sems.at[5])
    for copy in (got_copy, place_copy, term_copy, gate_copy, w_copy, cand_copy):
        copy.start()
    got_copy.wait()
    place_copy.wait()
    place = own_ref[:, 3 * width : 3 * width + slots]
    parts = weave(got_ref[:, 0].astype(F32), got_ref[:, 1].astype(F32))
    history = [dot(place, part.reshape(slots, half).astype(BF16)) for part in parts]
    term_copy.wait()
    term = own_ref[:, :width].astype(F32) + own_ref[:, width : 2 * width].astype(F32)
    attended = jnp.concatenate(history, 1) + term
    mean = jnp.sum(attended, 1, keepdims=True) / width
    centred = attended - mean
    var = jnp.sum(centred * centred, 1, keepdims=True) / width
    scaled = centred * lax.rsqrt(var + 1e-05)
    gate_copy.wait()
    normed = (scaled * own_ref[:, 2 * width : 3 * width].astype(F32)).astype(BF16)
    w_copy.wait()
    cand_copy.wait()
    pieces = out_sems.shape[0]
    count = cand_ref.shape[0] // pieces
    outs = []
    for index in range(pieces):
        span = slice(index * count, (index + 1) * count)
        result = cand_ref[span].astype(F32) + dot(normed[span], w_ref[...])
        out_ref[span] = result.astype(BF16)
        block = pl.ds(index * count, count)
        copy = pltpu.make_async_copy(out_ref.at[block], out_hbm.at[block], out_sems.at[index])
        copy.start()
        outs.append(copy)
    for copy in outs:
        copy.wait()


def tail(got, own, candidates, w_out):
    rows, width = candidates.shape
    sources = (got, own, candidates, w_out)
    return pl.pallas_call(
        tail_kernel,
        in_specs=[pl.BlockSpec(memory_space=pl.ANY)] * 4,
        out_specs=pl.BlockSpec(memory_space=pl.ANY),
        out_shape=jax.ShapeDtypeStruct((rows, width), BF16),
        scratch_shapes=[pltpu.VMEM(source.shape, source.dtype) for source in sources]
        + [
            pltpu.VMEM((rows, width), BF16),
            pltpu.SemaphoreType.DMA((6,)),
            pltpu.SemaphoreType.DMA((2,)),
        ],
        compiler_params=params(51),
        cost_estimate=pl.CostEstimate(
            flops=2 * rows * width * (width + got.shape[0] * 8), bytes_accessed=6 << 20, transcendentals=rows
        ),
        name="tail",
    )(*sources)


def exchange(rows):
    tiles, pair, eight, half = rows.shape
    flat = rows.reshape(tiles * pair, eight, half)
    return lax.all_to_all(flat, "serve", split_axis=0, concat_axis=0, tiled=True).reshape(rows.shape)


def per_device(history, candidates, cand_user, hist_len, w_uvqk, w_out):
    users = lax.axis_size("serve")
    outgoing, place = front(cand_user, candidates, w_uvqk, users)
    other = lax.ppermute(history, "rep", [(0, 1), (1, 0)])
    outgoing, history, place = lax.optimization_barrier((outgoing, history, place))
    received = exchange(outgoing)
    info = jnp.concatenate([hist_len, lax.axis_index("rep").astype(jnp.int32)[None]])
    keys, values = keys_vals(info, history, other, w_uvqk)
    own = own_part(candidates, w_uvqk, place)
    returned = exchange(attention(received, keys, values))
    return tail(returned, own, candidates, w_out)


def solution(mesh):
    placed = (
        P(("serve", "rep"), None),
        P(("serve", "rep"), None),
        P(("serve", "rep"), None),
        P("serve"),
        P(),
        P(),
    )
    return jax.shard_map(
        per_device, mesh=mesh, in_specs=placed, out_specs=P(("serve", "rep"), None), check_vma=False
    )
```

```python
import functools
import math

import jax
import jax.numpy as jnp
from jax import lax
from jax.experimental import pallas as pl
from jax.experimental.pallas import tpu as pltpu
from jax.sharding import PartitionSpec as P

HEADS = 8
CAP = 4
BF16 = jnp.bfloat16
F32 = jnp.float32


def silu(x):
    y = 0.5 * x
    return y + y * jnp.tanh(y)


def dot(a, b):
    return jnp.dot(a, b, preferred_element_type=F32)


def turn(matrix, identity):
    turned = lax.dot_general(matrix, identity, (((0,), (0,)), ((), ())), preferred_element_type=F32)
    return turned.astype(BF16)


def weave(first, second):
    low = lax.broadcasted_iota(jnp.int32, first.shape, 1) < 4
    even = jnp.where(low, first, pltpu.roll(second, 4, 1))
    odd = jnp.where(low, pltpu.roll(first, 4, 1), second)
    return even, odd


def params(limit=60):
    return pltpu.CompilerParams(vmem_limit_bytes=limit << 20)


def front_kernel(
    user_hbm, cand_hbm, w_hbm, out_hbm, place_hbm, user_ref, cand_ref, w_ref, out_ref, place_ref, in_sems, out_sems
):
    slots, rows = place_ref.shape
    users = slots // CAP
    width = cand_ref.shape[1]
    parts, depth, _ = w_ref.shape
    copies = [
        pltpu.make_async_copy(user_hbm, user_ref, in_sems.at[0]),
        pltpu.make_async_copy(cand_hbm, cand_ref, in_sems.at[1]),
    ]
    for index in range(parts):
        source = w_hbm.at[pl.ds(index * depth, depth), pl.ds(2 * width, width)]
        copies.append(pltpu.make_async_copy(source, w_ref.at[index], in_sems.at[2 + index]))
    for copy in copies:
        copy.start()

    copies[0].wait()
    ids = user_ref[...]
    one_hot = jnp.where(ids == lax.broadcasted_iota(jnp.int32, (users, rows), 0), 1.0, 0.0)
    earlier = jnp.where(
        lax.broadcasted_iota(jnp.int32, (rows, rows), 0)
        < lax.broadcasted_iota(jnp.int32, (rows, rows), 1),
        1.0,
        0.0,
    )
    before = dot(one_hot.astype(BF16), earlier.astype(BF16))
    rank = jnp.sum(before * one_hot, 0, keepdims=True).astype(jnp.int32)
    slot = ids * CAP + rank
    place = jnp.where(slot == lax.broadcasted_iota(jnp.int32, (slots, rows), 0), 1.0, 0.0).astype(BF16)
    place_ref[...] = place
    outs = [pltpu.make_async_copy(place_ref, place_hbm, out_sems.at[0])]
    outs[0].start()

    copies[1].wait()
    total = None
    for index in range(parts):
        copies[2 + index].wait()
        term = dot(cand_ref[:, index * depth : (index + 1) * depth], w_ref[index])
        total = term if total is None else total + term
    query = silu(total).astype(BF16)
    half = width // 2
    pieces = out_sems.shape[0] - 1
    count = slots // pieces
    tiles = count // 8
    for index in range(pieces):
        moved = dot(place[index * count : (index + 1) * count], query).reshape(tiles, 8, width)
        even, odd = weave(moved[:, :, :half], moved[:, :, half:])
        span = pl.ds(index * tiles, tiles)
        out_ref[span, 0] = even.astype(BF16)
        out_ref[span, 1] = odd.astype(BF16)
        copy = pltpu.make_async_copy(out_ref.at[span], out_hbm.at[span], out_sems.at[1 + index])
        copy.start()
        outs.append(copy)
    for copy in outs:
        copy.wait()


def front(cand_user, candidates, w_uvqk, users):
    rows, width = candidates.shape
    half = width // 2
    slots = users * CAP
    parts = 4
    pieces = 4
    whole = pl.BlockSpec(memory_space=pl.ANY)
    tiles = (slots // 8, 2, 8, half)
    return pl.pallas_call(
        front_kernel,
        in_specs=[whole] * 3,
        out_specs=[whole] * 2,
        out_shape=[
            jax.ShapeDtypeStruct(tiles, BF16),
            jax.ShapeDtypeStruct((slots, rows), BF16),
        ],
        scratch_shapes=[
            pltpu.VMEM((1, rows), jnp.int32),
            pltpu.VMEM((rows, width), BF16),
            pltpu.VMEM((parts, width // parts, width), BF16),
            pltpu.VMEM(tiles, BF16),
            pltpu.VMEM((slots, rows), BF16),
            pltpu.SemaphoreType.DMA((parts + 2,)),
            pltpu.SemaphoreType.DMA((pieces + 1,)),
        ],
        compiler_params=params(),
        cost_estimate=pl.CostEstimate(
            flops=2 * rows * width * (width + slots), bytes_accessed=5 << 20, transcendentals=rows * width
        ),
        name="front",
    )(cand_user.reshape(1, rows), candidates, w_uvqk)


def keys_vals_kernel(steps, info_ref, own_ref, other_ref, w_ref, key_ref, value_ref):
    count = own_ref.shape[0]
    weight = w_ref[...]
    for part, ref in enumerate((own_ref, other_ref)):
        result = silu(dot(ref[...], weight))
        span = slice(part * count, (part + 1) * count)

        @pl.when(pl.program_id(0) < steps)
        def _():
            row = lax.broadcasted_iota(jnp.int32, (count, count), 0)
            column = lax.broadcasted_iota(jnp.int32, (count, count), 1)
            identity = jnp.where(row == column, 1.0, 0.0).astype(BF16)
            key_ref[:, span] = turn(result.astype(BF16), identity)

        @pl.when(pl.program_id(0) >= steps)
        def _():
            start = jnp.where(info_ref[1] == part, 0, count)
            event = start + lax.broadcasted_iota(jnp.int32, result.shape, 0)
            value = jnp.where(event < info_ref[0], result, 0.0).astype(BF16)
            head_size = value_ref.shape[2]
            for head in range(value_ref.shape[0]):
                value_ref[head, span] = value[:, head * head_size : (head + 1) * head_size]


def keys_vals(info, own, other, w_uvqk):
    count, width = own.shape
    block = min(256, width)
    steps = width // block
    return pl.pallas_call(
        functools.partial(keys_vals_kernel, steps),
        grid=(2 * steps,),
        in_specs=[
            pl.BlockSpec(memory_space=pltpu.SMEM),
            pl.BlockSpec((count, width), lambda j: (0, 0)),
            pl.BlockSpec((count, width), lambda j: (0, 0)),
            pl.BlockSpec((width, block), lambda j: (0, jnp.where(j < steps, 3 * steps + j, j))),
        ],
        out_specs=[
            pl.BlockSpec((block, 2 * count), lambda j: (jnp.minimum(j, steps - 1), 0)),
            pl.BlockSpec((HEADS // steps, 2 * count, width // HEADS), lambda j: (jnp.maximum(j - steps, 0), 0, 0)),
        ],
        out_shape=[
            jax.ShapeDtypeStruct((width, 2 * count), BF16),
            jax.ShapeDtypeStruct((HEADS, 2 * count, width // HEADS), BF16),
        ],
        compiler_params=params(),
        cost_estimate=pl.CostEstimate(
            flops=8 * count * width * width, bytes_accessed=10 << 20, transcendentals=4 * count * width
        ),
        name="keys_vals",
    )(info, own, other, w_uvqk)


def attention_kernel(got_ref, key_hbm, value_hbm, out_hbm, key_ref, value_ref, out_ref, in_sems, out_sems):
    tiles, _, _, half = got_ref.shape
    slots = tiles * 8
    head_size = 2 * half // HEADS
    pairs = HEADS // 2
    copies = {}
    for pair in range(pairs):
        for head in (pair, pairs + pair):
            rows = pl.ds(head * head_size, head_size)
            copies[head] = (
                pltpu.make_async_copy(key_hbm.at[rows], key_ref.at[head], in_sems.at[head]),
                pltpu.make_async_copy(value_hbm.at[head], value_ref.at[head], in_sems.at[HEADS + head]),
            )
            for copy in copies[head]:
                copy.start()
    scale = 0.5 / math.sqrt(head_size)
    outs = []
    for group in ((0,), (1, 2, 3)):
        for pair in group:
            for head in (pair, pairs + pair):
                for copy in copies[head]:
                    copy.wait()
        for pair in group:
            columns = pl.ds(pair * head_size, head_size)
            queries = weave(got_ref[:, 0, :, columns].astype(F32), got_ref[:, 1, :, columns].astype(F32))
            results = []
            for query, head in zip(queries, (pair, pairs + pair)):
                rows = query.reshape(slots, head_size).astype(BF16)
                y = dot(rows, key_ref[head]) * scale
                weights = (y + y * jnp.tanh(y)).astype(BF16)
                results.append(dot(weights, value_ref[head]).reshape(tiles, 8, head_size))
            even, odd = weave(*results)
            out_ref[:, 0, :, columns] = even.astype(BF16)
            out_ref[:, 1, :, columns] = odd.astype(BF16)
            copy = pltpu.make_async_copy(
                out_ref.at[:, :, :, columns], out_hbm.at[:, :, :, columns], out_sems.at[pair]
            )
            copy.start()
            outs.append(copy)
    for copy in outs:
        copy.wait()


def attention(got, keys, values):
    tiles, _, _, half = got.shape
    slots = tiles * 8
    heads, events, head_size = values.shape
    whole = pl.BlockSpec(memory_space=pl.ANY)
    return pl.pallas_call(
        attention_kernel,
        in_specs=[pl.BlockSpec(memory_space=pltpu.VMEM), whole, whole],
        out_specs=whole,
        out_shape=jax.ShapeDtypeStruct(got.shape, BF16),
        scratch_shapes=[
            pltpu.VMEM((heads, head_size, events), BF16),
            pltpu.VMEM((heads, events, head_size), BF16),
            pltpu.VMEM(got.shape, BF16),
            pltpu.SemaphoreType.DMA((2 * heads,)),
            pltpu.SemaphoreType.DMA((heads // 2,)),
        ],
        compiler_params=params(50),
        cost_estimate=pl.CostEstimate(
            flops=8 * slots * events * half,
            bytes_accessed=6 << 20,
            transcendentals=slots * events * heads,
        ),
        name="attention",
    )(got, keys, values)


def own_kernel(head_size, cand_ref, wg_ref, wv_ref, wq_ref, wk_ref, place_ref, out_ref):
    step = pl.program_id(0)
    block = wg_ref.shape[1]
    rows, width = cand_ref.shape
    slots = place_ref.shape[0]

    @pl.when(step == 0)
    def _():
        out_ref[:, 3 * width : 3 * width + slots] = place_ref[...].astype(F32).T.astype(BF16)

    cand = cand_ref[...]
    gate, value, query, key = (
        silu(dot(cand, ref[...])).astype(BF16) for ref in (wg_ref, wv_ref, wq_ref, wk_ref)
    )
    product = query.astype(F32) * key.astype(F32)
    value = value.astype(F32)
    terms = []
    for start in range(0, block, head_size):
        columns = slice(start, start + head_size)
        score = jnp.sum(product[:, columns], 1, keepdims=True) / math.sqrt(head_size)
        terms.append(silu(score) * value[:, columns])
    term = jnp.concatenate(terms, 1)
    high = term.astype(BF16)
    low = (term - high.astype(F32)).astype(BF16)
    for index, array in enumerate((high, low, gate)):
        start = pl.multiple_of(index * width + step * block, block)
        out_ref[:, pl.ds(start, block)] = array


def own_part(candidates, w_uvqk, place):
    rows, width = candidates.shape
    slots = place.shape[0]
    block = 256
    steps = width // block
    return pl.pallas_call(
        functools.partial(own_kernel, width // HEADS),
        grid=(steps,),
        in_specs=[
            pl.BlockSpec((rows, width), lambda j: (0, 0)),
            pl.BlockSpec((width, block), lambda j: (0, j)),
            pl.BlockSpec((width, block), lambda j: (0, steps + j)),
            pl.BlockSpec((width, block), lambda j: (0, 2 * steps + j)),
            pl.BlockSpec((width, block), lambda j: (0, 3 * steps + j)),
            pl.BlockSpec((slots, rows), lambda j: (0, 0)),
        ],
        out_specs=pl.BlockSpec((rows, 3 * width + slots), lambda j: (0, 0)),
        out_shape=jax.ShapeDtypeStruct((rows, 3 * width + slots), BF16),
        compiler_params=params(50),
        cost_estimate=pl.CostEstimate(
            flops=8 * rows * width * width, bytes_accessed=11 << 20, transcendentals=4 * rows * width
        ),
        name="own_part",
    )(candidates, w_uvqk, w_uvqk, w_uvqk, w_uvqk, place)


def tail_kernel(got_ref, own_ref, cand_ref, w_hbm, out_hbm, w_ref, out_ref, in_sem, out_sems):
    tiles, _, _, half = got_ref.shape
    width = 2 * half
    slots = tiles * 8
    w_copy = pltpu.make_async_copy(w_hbm, w_ref, in_sem.at[0])
    w_copy.start()
    place = own_ref[:, 3 * width : 3 * width + slots]
    parts = weave(got_ref[:, 0].astype(F32), got_ref[:, 1].astype(F32))
    history = [dot(place, part.reshape(slots, half).astype(BF16)) for part in parts]
    term = own_ref[:, :width].astype(F32) + own_ref[:, width : 2 * width].astype(F32)
    attended = jnp.concatenate(history, 1) + term
    mean = jnp.sum(attended, 1, keepdims=True) / width
    centred = attended - mean
    var = jnp.sum(centred * centred, 1, keepdims=True) / width
    scaled = centred * lax.rsqrt(var + 1e-05)
    normed = (scaled * own_ref[:, 2 * width : 3 * width].astype(F32)).astype(BF16)
    w_copy.wait()
    pieces = out_sems.shape[0]
    count = cand_ref.shape[0] // pieces
    outs = []
    for index in range(pieces):
        span = slice(index * count, (index + 1) * count)
        result = cand_ref[span].astype(F32) + dot(normed[span], w_ref[...])
        out_ref[span] = result.astype(BF16)
        block = pl.ds(index * count, count)
        copy = pltpu.make_async_copy(out_ref.at[block], out_hbm.at[block], out_sems.at[index])
        copy.start()
        outs.append(copy)
    for copy in outs:
        copy.wait()


def tail(got, own, candidates, w_out):
    rows, width = candidates.shape
    inside = pl.BlockSpec(memory_space=pltpu.VMEM)
    return pl.pallas_call(
        tail_kernel,
        in_specs=[inside] * 3 + [pl.BlockSpec(memory_space=pl.ANY)],
        out_specs=pl.BlockSpec(memory_space=pl.ANY),
        out_shape=jax.ShapeDtypeStruct((rows, width), BF16),
        scratch_shapes=[
            pltpu.VMEM(w_out.shape, BF16),
            pltpu.VMEM((rows, width), BF16),
            pltpu.SemaphoreType.DMA((1,)),
            pltpu.SemaphoreType.DMA((2,)),
        ],
        compiler_params=params(50),
        cost_estimate=pl.CostEstimate(
            flops=2 * rows * width * (width + got.shape[0] * 8), bytes_accessed=6 << 20, transcendentals=rows
        ),
        name="tail",
    )(got, own, candidates, w_out)


def exchange(rows):
    tiles, pair, eight, half = rows.shape
    flat = rows.reshape(tiles * pair, eight, half)
    return lax.all_to_all(flat, "serve", split_axis=0, concat_axis=0, tiled=True).reshape(rows.shape)


def per_device(history, candidates, cand_user, hist_len, w_uvqk, w_out):
    users = lax.axis_size("serve")
    outgoing, place = front(cand_user, candidates, w_uvqk, users)
    other = lax.ppermute(history, "rep", [(0, 1), (1, 0)])
    outgoing, history, place = lax.optimization_barrier((outgoing, history, place))
    received = exchange(outgoing)
    info = jnp.concatenate([hist_len, lax.axis_index("rep").astype(jnp.int32)[None]])
    keys, values = keys_vals(info, history, other, w_uvqk)
    own = own_part(candidates, w_uvqk, place)
    returned = exchange(attention(received, keys, values))
    return tail(returned, own, candidates, w_out)


def solution(mesh):
    placed = (
        P(("serve", "rep"), None),
        P(("serve", "rep"), None),
        P(("serve", "rep"), None),
        P("serve"),
        P(),
        P(),
    )
    return jax.shard_map(
        per_device, mesh=mesh, in_specs=placed, out_specs=P(("serve", "rep"), None), check_vma=False
    )
```

```python
import functools
import math

import jax
import jax.numpy as jnp
from jax import lax
from jax.experimental import pallas as pl
from jax.experimental.pallas import tpu as pltpu
from jax.sharding import PartitionSpec as P

HEADS = 8
CAP = 4
BF16 = jnp.bfloat16
F32 = jnp.float32


def silu(x):
    y = 0.5 * x
    return y + y * jnp.tanh(y)


def dot(a, b):
    return jnp.dot(a, b, preferred_element_type=F32)


def turn(matrix, identity):
    turned = lax.dot_general(matrix, identity, (((0,), (0,)), ((), ())), preferred_element_type=F32)
    return turned.astype(BF16)


def weave(first, second):
    low = lax.broadcasted_iota(jnp.int32, first.shape, 1) < 4
    even = jnp.where(low, first, pltpu.roll(second, 4, 1))
    odd = jnp.where(low, pltpu.roll(first, 4, 1), second)
    return even, odd


def params(limit=60):
    return pltpu.CompilerParams(vmem_limit_bytes=limit << 20)


def front_kernel(
    user_hbm, cand_hbm, w_hbm, out_hbm, place_hbm, user_ref, cand_ref, w_ref, out_ref, place_ref, in_sems, out_sems
):
    slots, rows = place_ref.shape
    users = slots // CAP
    width = cand_ref.shape[1]
    parts, depth, _ = w_ref.shape
    copies = [
        pltpu.make_async_copy(user_hbm, user_ref, in_sems.at[0]),
        pltpu.make_async_copy(cand_hbm, cand_ref, in_sems.at[1]),
    ]
    for index in range(parts):
        source = w_hbm.at[pl.ds(index * depth, depth), pl.ds(2 * width, width)]
        copies.append(pltpu.make_async_copy(source, w_ref.at[index], in_sems.at[2 + index]))
    for copy in copies:
        copy.start()

    copies[0].wait()
    ids = user_ref[...]
    one_hot = jnp.where(ids == lax.broadcasted_iota(jnp.int32, (users, rows), 0), 1.0, 0.0)
    earlier = jnp.where(
        lax.broadcasted_iota(jnp.int32, (rows, rows), 0)
        < lax.broadcasted_iota(jnp.int32, (rows, rows), 1),
        1.0,
        0.0,
    )
    before = dot(one_hot.astype(BF16), earlier.astype(BF16))
    rank = jnp.sum(before * one_hot, 0, keepdims=True).astype(jnp.int32)
    slot = ids * CAP + rank
    place = jnp.where(slot == lax.broadcasted_iota(jnp.int32, (slots, rows), 0), 1.0, 0.0).astype(BF16)
    place_ref[...] = place
    outs = [pltpu.make_async_copy(place_ref, place_hbm, out_sems.at[0])]
    outs[0].start()

    copies[1].wait()
    total = None
    for index in range(parts):
        copies[2 + index].wait()
        term = dot(cand_ref[:, index * depth : (index + 1) * depth], w_ref[index])
        total = term if total is None else total + term
    query = silu(total).astype(BF16)
    half = width // 2
    pieces = out_sems.shape[0] - 1
    count = slots // pieces
    tiles = count // 8
    for index in range(pieces):
        moved = dot(place[index * count : (index + 1) * count], query).reshape(tiles, 8, width)
        even, odd = weave(moved[:, :, :half], moved[:, :, half:])
        span = pl.ds(index * tiles, tiles)
        out_ref[span, 0] = even.astype(BF16)
        out_ref[span, 1] = odd.astype(BF16)
        copy = pltpu.make_async_copy(out_ref.at[span], out_hbm.at[span], out_sems.at[1 + index])
        copy.start()
        outs.append(copy)
    for copy in outs:
        copy.wait()


def front(cand_user, candidates, w_uvqk, users):
    rows, width = candidates.shape
    half = width // 2
    slots = users * CAP
    parts = 4
    pieces = 4
    whole = pl.BlockSpec(memory_space=pl.ANY)
    tiles = (slots // 8, 2, 8, half)
    return pl.pallas_call(
        front_kernel,
        in_specs=[whole] * 3,
        out_specs=[whole] * 2,
        out_shape=[
            jax.ShapeDtypeStruct(tiles, BF16),
            jax.ShapeDtypeStruct((slots, rows), BF16),
        ],
        scratch_shapes=[
            pltpu.VMEM((1, rows), jnp.int32),
            pltpu.VMEM((rows, width), BF16),
            pltpu.VMEM((parts, width // parts, width), BF16),
            pltpu.VMEM(tiles, BF16),
            pltpu.VMEM((slots, rows), BF16),
            pltpu.SemaphoreType.DMA((parts + 2,)),
            pltpu.SemaphoreType.DMA((pieces + 1,)),
        ],
        compiler_params=params(),
        cost_estimate=pl.CostEstimate(
            flops=2 * rows * width * (width + slots), bytes_accessed=5 << 20, transcendentals=rows * width
        ),
        name="front",
    )(cand_user.reshape(1, rows), candidates, w_uvqk)


def keys_vals_kernel(steps, info_ref, own_ref, w_ref, key_ref, value_ref):
    count = own_ref.shape[0]
    result = silu(dot(own_ref[...], w_ref[...]))

    @pl.when(pl.program_id(0) < steps)
    def _():
        row = lax.broadcasted_iota(jnp.int32, (count, count), 0)
        column = lax.broadcasted_iota(jnp.int32, (count, count), 1)
        identity = jnp.where(row == column, 1.0, 0.0).astype(BF16)
        key_ref[...] = turn(result.astype(BF16), identity)

    @pl.when(pl.program_id(0) >= steps)
    def _():
        event = info_ref[1] * count + lax.broadcasted_iota(jnp.int32, result.shape, 0)
        value = jnp.where(event < info_ref[0], result, 0.0).astype(BF16)
        head_size = value_ref.shape[2]
        for head in range(value_ref.shape[0]):
            value_ref[head] = value[:, head * head_size : (head + 1) * head_size]


def keys_vals(info, own, w_uvqk):
    count, width = own.shape
    block = min(256, width)
    steps = width // block
    return pl.pallas_call(
        functools.partial(keys_vals_kernel, steps),
        grid=(2 * steps,),
        in_specs=[
            pl.BlockSpec(memory_space=pltpu.SMEM),
            pl.BlockSpec((count, width), lambda j: (0, 0)),
            pl.BlockSpec((width, block), lambda j: (0, jnp.where(j < steps, 3 * steps + j, j))),
        ],
        out_specs=[
            pl.BlockSpec((block, count), lambda j: (jnp.minimum(j, steps - 1), 0)),
            pl.BlockSpec((HEADS // steps, count, width // HEADS), lambda j: (jnp.maximum(j - steps, 0), 0, 0)),
        ],
        out_shape=[
            jax.ShapeDtypeStruct((width, count), BF16),
            jax.ShapeDtypeStruct((HEADS, count, width // HEADS), BF16),
        ],
        compiler_params=params(),
        cost_estimate=pl.CostEstimate(
            flops=4 * count * width * width, bytes_accessed=7 << 20, transcendentals=2 * count * width
        ),
        name="keys_vals",
    )(info, own, w_uvqk)


def attention_kernel(
    got_ref, key0_hbm, key1_hbm, value0_hbm, value1_hbm, out_hbm, key_ref, value_ref, out_ref, in_sems, out_sems):
    tiles, _, _, half = got_ref.shape
    slots = tiles * 8
    head_size = 2 * half // HEADS
    pairs = HEADS // 2
    key_hbms, value_hbms = (key0_hbm, key1_hbm), (value0_hbm, value1_hbm)
    copies = {}
    count = key_hbms[0].shape[1]
    for pair in range(pairs):
        for head in (pair, pairs + pair):
            rows = pl.ds(head * head_size, head_size)
            copies[head] = []
            for part in range(2):
                span = pl.ds(part * count, count)
                sem = in_sems.at[head, part]
                copies[head].append(
                    pltpu.make_async_copy(key_hbms[part].at[rows], key_ref.at[head, :, span], sem.at[0])
                )
                copies[head].append(
                    pltpu.make_async_copy(value_hbms[part].at[head], value_ref.at[head, span], sem.at[1])
                )
            for copy in copies[head]:
                copy.start()
    scale = 0.5 / math.sqrt(head_size)
    outs = []
    for group in ((0,), (1, 2, 3)):
        for pair in group:
            for head in (pair, pairs + pair):
                for copy in copies[head]:
                    copy.wait()
        for pair in group:
            columns = pl.ds(pair * head_size, head_size)
            queries = weave(got_ref[:, 0, :, columns].astype(F32), got_ref[:, 1, :, columns].astype(F32))
            results = []
            for query, head in zip(queries, (pair, pairs + pair)):
                rows = query.reshape(slots, head_size).astype(BF16)
                y = dot(rows, key_ref[head]) * scale
                weights = (y + y * jnp.tanh(y)).astype(BF16)
                results.append(dot(weights, value_ref[head]).reshape(tiles, 8, head_size))
            even, odd = weave(*results)
            out_ref[:, 0, :, columns] = even.astype(BF16)
            out_ref[:, 1, :, columns] = odd.astype(BF16)
            copy = pltpu.make_async_copy(
                out_ref.at[:, :, :, columns], out_hbm.at[:, :, :, columns], out_sems.at[pair]
            )
            copy.start()
            outs.append(copy)
    for copy in outs:
        copy.wait()


def attention(got, keys, values):
    tiles, _, _, half = got.shape
    slots = tiles * 8
    heads, count, head_size = values[0].shape
    events = 2 * count
    whole = pl.BlockSpec(memory_space=pl.ANY)
    return pl.pallas_call(
        attention_kernel,
        in_specs=[pl.BlockSpec(memory_space=pltpu.VMEM)] + [whole] * 4,
        out_specs=whole,
        out_shape=jax.ShapeDtypeStruct(got.shape, BF16),
        scratch_shapes=[
            pltpu.VMEM((heads, head_size, events), BF16),
            pltpu.VMEM((heads, events, head_size), BF16),
            pltpu.VMEM(got.shape, BF16),
            pltpu.SemaphoreType.DMA((heads, 2, 2)),
            pltpu.SemaphoreType.DMA((heads // 2,)),
        ],
        compiler_params=params(51),
        cost_estimate=pl.CostEstimate(
            flops=8 * slots * events * half,
            bytes_accessed=6 << 20,
            transcendentals=slots * events * heads,
        ),
        name="attention",
    )(got, *keys, *values)


def own_kernel(head_size, cand_ref, wg_ref, wv_ref, wq_ref, wk_ref, place_ref, out_ref):
    step = pl.program_id(0)
    block = wg_ref.shape[1]
    rows, width = cand_ref.shape
    slots = place_ref.shape[0]

    @pl.when(step == 0)
    def _():
        out_ref[:, 3 * width : 3 * width + slots] = place_ref[...].astype(F32).T.astype(BF16)

    cand = cand_ref[...]
    gate, value, query, key = (
        silu(dot(cand, ref[...])).astype(BF16) for ref in (wg_ref, wv_ref, wq_ref, wk_ref)
    )
    product = query.astype(F32) * key.astype(F32)
    value = value.astype(F32)
    terms = []
    for start in range(0, block, head_size):
        columns = slice(start, start + head_size)
        score = jnp.sum(product[:, columns], 1, keepdims=True) / math.sqrt(head_size)
        terms.append(silu(score) * value[:, columns])
    term = jnp.concatenate(terms, 1)
    high = term.astype(BF16)
    low = (term - high.astype(F32)).astype(BF16)
    for index, array in enumerate((high, low, gate)):
        start = pl.multiple_of(index * width + step * block, block)
        out_ref[:, pl.ds(start, block)] = array


def own_part(candidates, w_uvqk, place):
    rows, width = candidates.shape
    slots = place.shape[0]
    block = 256
    steps = width // block
    return pl.pallas_call(
        functools.partial(own_kernel, width // HEADS),
        grid=(steps,),
        in_specs=[
            pl.BlockSpec((rows, width), lambda j: (0, 0)),
            pl.BlockSpec((width, block), lambda j: (0, j)),
            pl.BlockSpec((width, block), lambda j: (0, steps + j)),
            pl.BlockSpec((width, block), lambda j: (0, 2 * steps + j)),
            pl.BlockSpec((width, block), lambda j: (0, 3 * steps + j)),
            pl.BlockSpec((slots, rows), lambda j: (0, 0)),
        ],
        out_specs=pl.BlockSpec((rows, 3 * width + slots), lambda j: (0, 0)),
        out_shape=jax.ShapeDtypeStruct((rows, 3 * width + slots), BF16),
        compiler_params=params(50),
        cost_estimate=pl.CostEstimate(
            flops=8 * rows * width * width, bytes_accessed=11 << 20, transcendentals=4 * rows * width
        ),
        name="own_part",
    )(candidates, w_uvqk, w_uvqk, w_uvqk, w_uvqk, place)


def tail_kernel(got_ref, own_ref, cand_ref, w_hbm, out_hbm, w_ref, out_ref, in_sem, out_sems):
    tiles, _, _, half = got_ref.shape
    width = 2 * half
    slots = tiles * 8
    w_copy = pltpu.make_async_copy(w_hbm, w_ref, in_sem.at[0])
    w_copy.start()
    place = own_ref[:, 3 * width : 3 * width + slots]
    parts = weave(got_ref[:, 0].astype(F32), got_ref[:, 1].astype(F32))
    history = [dot(place, part.reshape(slots, half).astype(BF16)) for part in parts]
    term = own_ref[:, :width].astype(F32) + own_ref[:, width : 2 * width].astype(F32)
    attended = jnp.concatenate(history, 1) + term
    mean = jnp.sum(attended, 1, keepdims=True) / width
    centred = attended - mean
    var = jnp.sum(centred * centred, 1, keepdims=True) / width
    scaled = centred * lax.rsqrt(var + 1e-05)
    normed = (scaled * own_ref[:, 2 * width : 3 * width].astype(F32)).astype(BF16)
    w_copy.wait()
    pieces = out_sems.shape[0]
    count = cand_ref.shape[0] // pieces
    outs = []
    for index in range(pieces):
        span = slice(index * count, (index + 1) * count)
        result = cand_ref[span].astype(F32) + dot(normed[span], w_ref[...])
        out_ref[span] = result.astype(BF16)
        block = pl.ds(index * count, count)
        copy = pltpu.make_async_copy(out_ref.at[block], out_hbm.at[block], out_sems.at[index])
        copy.start()
        outs.append(copy)
    for copy in outs:
        copy.wait()


def tail(got, own, candidates, w_out):
    rows, width = candidates.shape
    inside = pl.BlockSpec(memory_space=pltpu.VMEM)
    return pl.pallas_call(
        tail_kernel,
        in_specs=[inside] * 3 + [pl.BlockSpec(memory_space=pl.ANY)],
        out_specs=pl.BlockSpec(memory_space=pl.ANY),
        out_shape=jax.ShapeDtypeStruct((rows, width), BF16),
        scratch_shapes=[
            pltpu.VMEM(w_out.shape, BF16),
            pltpu.VMEM((rows, width), BF16),
            pltpu.SemaphoreType.DMA((1,)),
            pltpu.SemaphoreType.DMA((2,)),
        ],
        compiler_params=params(50),
        cost_estimate=pl.CostEstimate(
            flops=2 * rows * width * (width + got.shape[0] * 8), bytes_accessed=6 << 20, transcendentals=rows
        ),
        name="tail",
    )(got, own, candidates, w_out)


def exchange(rows):
    tiles, pair, eight, half = rows.shape
    flat = rows.reshape(tiles * pair, eight, half)
    return lax.all_to_all(flat, "serve", split_axis=0, concat_axis=0, tiled=True).reshape(rows.shape)


def per_device(history, candidates, cand_user, hist_len, w_uvqk, w_out):
    users = lax.axis_size("serve")
    outgoing, place = front(cand_user, candidates, w_uvqk, users)
    outgoing, history, place = lax.optimization_barrier((outgoing, history, place))
    received = exchange(outgoing)
    info = jnp.concatenate([hist_len, lax.axis_index("rep").astype(jnp.int32)[None]])
    key, value = keys_vals(info, history, w_uvqk)
    key, value, place = lax.optimization_barrier((key, value, place))
    other_key, other_value = (lax.ppermute(half, "rep", [(0, 1), (1, 0)]) for half in (key, value))
    own = own_part(candidates, w_uvqk, place)
    received, own = lax.optimization_barrier((received, own))
    returned = exchange(attention(received, (key, other_key), (value, other_value)))
    return tail(returned, own, candidates, w_out)


def solution(mesh):
    placed = (
        P(("serve", "rep"), None),
        P(("serve", "rep"), None),
        P(("serve", "rep"), None),
        P("serve"),
        P(),
        P(),
    )
    return jax.shard_map(
        per_device, mesh=mesh, in_specs=placed, out_specs=P(("serve", "rep"), None), check_vma=False
    )
```

```python
import functools
import math

import jax
import jax.numpy as jnp
from jax import lax
from jax.experimental import pallas as pl
from jax.experimental.pallas import tpu as pltpu
from jax.sharding import PartitionSpec as P

HEADS = 8
CAP = 4
BF16 = jnp.bfloat16
F32 = jnp.float32


def silu(x):
    y = 0.5 * x
    return y + y * jnp.tanh(y)


def dot(a, b):
    return jnp.dot(a, b, preferred_element_type=F32)


def turn(matrix, identity):
    turned = lax.dot_general(matrix, identity, (((0,), (0,)), ((), ())), preferred_element_type=F32)
    return turned.astype(BF16)


def weave(first, second):
    low = lax.broadcasted_iota(jnp.int32, first.shape, 1) < 4
    even = jnp.where(low, first, pltpu.roll(second, 4, 1))
    odd = jnp.where(low, pltpu.roll(first, 4, 1), second)
    return even, odd


def params(limit=60):
    return pltpu.CompilerParams(vmem_limit_bytes=limit << 20)


def front_kernel(
    user_hbm, cand_hbm, w_hbm, out_hbm, place_hbm, user_ref, cand_ref, w_ref, out_ref, place_ref, in_sems, out_sems
):
    slots, rows = place_ref.shape
    users = slots // CAP
    width = cand_ref.shape[1]
    parts, depth, _ = w_ref.shape
    copies = [
        pltpu.make_async_copy(user_hbm, user_ref, in_sems.at[0]),
        pltpu.make_async_copy(cand_hbm, cand_ref, in_sems.at[1]),
    ]
    for index in range(parts):
        source = w_hbm.at[pl.ds(index * depth, depth), pl.ds(2 * width, width)]
        copies.append(pltpu.make_async_copy(source, w_ref.at[index], in_sems.at[2 + index]))
    for copy in copies:
        copy.start()

    copies[0].wait()
    ids = user_ref[...]
    one_hot = jnp.where(ids == lax.broadcasted_iota(jnp.int32, (users, rows), 0), 1.0, 0.0)
    earlier = jnp.where(
        lax.broadcasted_iota(jnp.int32, (rows, rows), 0)
        < lax.broadcasted_iota(jnp.int32, (rows, rows), 1),
        1.0,
        0.0,
    )
    before = dot(one_hot.astype(BF16), earlier.astype(BF16))
    rank = jnp.sum(before * one_hot, 0, keepdims=True).astype(jnp.int32)
    slot = ids * CAP + rank
    place = jnp.where(slot == lax.broadcasted_iota(jnp.int32, (slots, rows), 0), 1.0, 0.0).astype(BF16)
    place_ref[...] = place
    outs = [pltpu.make_async_copy(place_ref, place_hbm, out_sems.at[0])]
    outs[0].start()

    copies[1].wait()
    total = None
    for index in range(parts):
        copies[2 + index].wait()
        term = dot(cand_ref[:, index * depth : (index + 1) * depth], w_ref[index])
        total = term if total is None else total + term
    query = silu(total).astype(BF16)
    half = width // 2
    pieces = out_sems.shape[0] - 1
    count = slots // pieces
    tiles = count // 8
    for index in range(pieces):
        moved = dot(place[index * count : (index + 1) * count], query).reshape(tiles, 8, width)
        even, odd = weave(moved[:, :, :half], moved[:, :, half:])
        span = pl.ds(index * tiles, tiles)
        out_ref[span, 0] = even.astype(BF16)
        out_ref[span, 1] = odd.astype(BF16)
        copy = pltpu.make_async_copy(out_ref.at[span], out_hbm.at[span], out_sems.at[1 + index])
        copy.start()
        outs.append(copy)
    for copy in outs:
        copy.wait()


def front(cand_user, candidates, w_uvqk, users):
    rows, width = candidates.shape
    half = width // 2
    slots = users * CAP
    parts = 4
    pieces = 4
    whole = pl.BlockSpec(memory_space=pl.ANY)
    tiles = (slots // 8, 2, 8, half)
    return pl.pallas_call(
        front_kernel,
        in_specs=[whole] * 3,
        out_specs=[whole] * 2,
        out_shape=[
            jax.ShapeDtypeStruct(tiles, BF16),
            jax.ShapeDtypeStruct((slots, rows), BF16),
        ],
        scratch_shapes=[
            pltpu.VMEM((1, rows), jnp.int32),
            pltpu.VMEM((rows, width), BF16),
            pltpu.VMEM((parts, width // parts, width), BF16),
            pltpu.VMEM(tiles, BF16),
            pltpu.VMEM((slots, rows), BF16),
            pltpu.SemaphoreType.DMA((parts + 2,)),
            pltpu.SemaphoreType.DMA((pieces + 1,)),
        ],
        compiler_params=params(),
        cost_estimate=pl.CostEstimate(
            flops=2 * rows * width * (width + slots), bytes_accessed=5 << 20, transcendentals=rows * width
        ),
        name="front",
    )(cand_user.reshape(1, rows), candidates, w_uvqk)


def keys_vals_kernel(steps, info_ref, own_ref, w_ref, key_ref, value_ref):
    count = own_ref.shape[0]
    result = silu(dot(own_ref[...], w_ref[...]))

    @pl.when(pl.program_id(0) < steps)
    def _():
        row = lax.broadcasted_iota(jnp.int32, (count, count), 0)
        column = lax.broadcasted_iota(jnp.int32, (count, count), 1)
        identity = jnp.where(row == column, 1.0, 0.0).astype(BF16)
        key_ref[...] = turn(result.astype(BF16), identity)

    @pl.when(pl.program_id(0) >= steps)
    def _():
        event = info_ref[1] * count + lax.broadcasted_iota(jnp.int32, result.shape, 0)
        value = jnp.where(event < info_ref[0], result, 0.0).astype(BF16)
        head_size = value_ref.shape[2]
        for head in range(value_ref.shape[0]):
            value_ref[head] = value[:, head * head_size : (head + 1) * head_size]


def keys_vals(info, own, w_uvqk):
    count, width = own.shape
    block = min(256, width)
    steps = width // block
    return pl.pallas_call(
        functools.partial(keys_vals_kernel, steps),
        grid=(2 * steps,),
        in_specs=[
            pl.BlockSpec(memory_space=pltpu.SMEM),
            pl.BlockSpec((count, width), lambda j: (0, 0)),
            pl.BlockSpec((width, block), lambda j: (0, jnp.where(j < steps, 3 * steps + j, j))),
        ],
        out_specs=[
            pl.BlockSpec((block, count), lambda j: (jnp.minimum(j, steps - 1), 0)),
            pl.BlockSpec((HEADS // steps, count, width // HEADS), lambda j: (jnp.maximum(j - steps, 0), 0, 0)),
        ],
        out_shape=[
            jax.ShapeDtypeStruct((width, count), BF16),
            jax.ShapeDtypeStruct((HEADS, count, width // HEADS), BF16),
        ],
        compiler_params=params(),
        cost_estimate=pl.CostEstimate(
            flops=4 * count * width * width, bytes_accessed=7 << 20, transcendentals=2 * count * width
        ),
        name="keys_vals",
    )(info, own, w_uvqk)


def attention_kernel(
    got_ref, key0_hbm, key1_hbm, value0_hbm, value1_hbm, out_ref, key_ref, value_ref, in_sems
):
    tiles, _, _, half = got_ref.shape
    slots = tiles * 8
    head_size = 2 * half // HEADS
    pairs = HEADS // 2
    key_hbms, value_hbms = (key0_hbm, key1_hbm), (value0_hbm, value1_hbm)
    copies = {}
    count = key_hbms[0].shape[1]
    for pair in range(pairs):
        for head in (pair, pairs + pair):
            rows = pl.ds(head * head_size, head_size)
            copies[head] = []
            for part in range(2):
                span = pl.ds(part * count, count)
                sem = in_sems.at[head, part]
                copies[head].append(
                    pltpu.make_async_copy(key_hbms[part].at[rows], key_ref.at[head, :, span], sem.at[0])
                )
                copies[head].append(
                    pltpu.make_async_copy(value_hbms[part].at[head], value_ref.at[head, span], sem.at[1])
                )
            for copy in copies[head]:
                copy.start()
    scale = 0.5 / math.sqrt(head_size)
    for group in ((0,), (1, 2, 3)):
        for pair in group:
            for head in (pair, pairs + pair):
                for copy in copies[head]:
                    copy.wait()
        for pair in group:
            columns = pl.ds(pair * head_size, head_size)
            queries = weave(got_ref[:, 0, :, columns].astype(F32), got_ref[:, 1, :, columns].astype(F32))
            results = []
            for query, head in zip(queries, (pair, pairs + pair)):
                rows = query.reshape(slots, head_size).astype(BF16)
                y = dot(rows, key_ref[head]) * scale
                weights = (y + y * jnp.tanh(y)).astype(BF16)
                results.append(dot(weights, value_ref[head]).reshape(tiles, 8, head_size))
            even, odd = weave(*results)
            out_ref[:, 0, :, columns] = even.astype(BF16)
            out_ref[:, 1, :, columns] = odd.astype(BF16)


def attention(got, keys, values):
    tiles, _, _, half = got.shape
    slots = tiles * 8
    heads, count, head_size = values[0].shape
    events = 2 * count
    whole = pl.BlockSpec(memory_space=pl.ANY)
    return pl.pallas_call(
        attention_kernel,
        in_specs=[pl.BlockSpec(memory_space=pltpu.VMEM)] + [whole] * 4,
        out_specs=pl.BlockSpec(memory_space=pltpu.VMEM),
        out_shape=jax.ShapeDtypeStruct(got.shape, BF16),
        scratch_shapes=[
            pltpu.VMEM((heads, head_size, events), BF16),
            pltpu.VMEM((heads, events, head_size), BF16),
            pltpu.SemaphoreType.DMA((heads, 2, 2)),
        ],
        compiler_params=params(51),
        cost_estimate=pl.CostEstimate(
            flops=8 * slots * events * half,
            bytes_accessed=6 << 20,
            transcendentals=slots * events * heads,
        ),
        name="attention",
    )(got, *keys, *values)


def own_kernel(head_size, cand_ref, wg_ref, wv_ref, wq_ref, wk_ref, place_ref, out_ref):
    step = pl.program_id(0)
    block = wg_ref.shape[1]
    rows, width = cand_ref.shape
    slots = place_ref.shape[0]

    @pl.when(step == 0)
    def _():
        out_ref[:, 3 * width : 3 * width + slots] = place_ref[...].astype(F32).T.astype(BF16)

    cand = cand_ref[...]
    gate, value, query, key = (
        silu(dot(cand, ref[...])).astype(BF16) for ref in (wg_ref, wv_ref, wq_ref, wk_ref)
    )
    product = query.astype(F32) * key.astype(F32)
    value = value.astype(F32)
    terms = []
    for start in range(0, block, head_size):
        columns = slice(start, start + head_size)
        score = jnp.sum(product[:, columns], 1, keepdims=True) / math.sqrt(head_size)
        terms.append(silu(score) * value[:, columns])
    term = jnp.concatenate(terms, 1)
    high = term.astype(BF16)
    low = (term - high.astype(F32)).astype(BF16)
    for index, array in enumerate((high, low, gate)):
        start = pl.multiple_of(index * width + step * block, block)
        out_ref[:, pl.ds(start, block)] = array


def own_part(candidates, w_uvqk, place):
    rows, width = candidates.shape
    slots = place.shape[0]
    block = 256
    steps = width // block
    return pl.pallas_call(
        functools.partial(own_kernel, width // HEADS),
        grid=(steps,),
        in_specs=[
            pl.BlockSpec((rows, width), lambda j: (0, 0)),
            pl.BlockSpec((width, block), lambda j: (0, j)),
            pl.BlockSpec((width, block), lambda j: (0, steps + j)),
            pl.BlockSpec((width, block), lambda j: (0, 2 * steps + j)),
            pl.BlockSpec((width, block), lambda j: (0, 3 * steps + j)),
            pl.BlockSpec((slots, rows), lambda j: (0, 0)),
        ],
        out_specs=pl.BlockSpec((rows, 3 * width + slots), lambda j: (0, 0)),
        out_shape=jax.ShapeDtypeStruct((rows, 3 * width + slots), BF16),
        compiler_params=params(50),
        cost_estimate=pl.CostEstimate(
            flops=8 * rows * width * width, bytes_accessed=11 << 20, transcendentals=4 * rows * width
        ),
        name="own_part",
    )(candidates, w_uvqk, w_uvqk, w_uvqk, w_uvqk, place)


def tail_kernel(got_ref, own_ref, cand_ref, w_hbm, out_hbm, w_ref, out_ref, in_sem, out_sems):
    tiles, _, _, half = got_ref.shape
    width = 2 * half
    slots = tiles * 8
    w_copy = pltpu.make_async_copy(w_hbm, w_ref, in_sem.at[0])
    w_copy.start()
    place = own_ref[:, 3 * width : 3 * width + slots]
    parts = weave(got_ref[:, 0].astype(F32), got_ref[:, 1].astype(F32))
    history = [dot(place, part.reshape(slots, half).astype(BF16)) for part in parts]
    term = own_ref[:, :width].astype(F32) + own_ref[:, width : 2 * width].astype(F32)
    attended = jnp.concatenate(history, 1) + term
    mean = jnp.sum(attended, 1, keepdims=True) / width
    centred = attended - mean
    var = jnp.sum(centred * centred, 1, keepdims=True) / width
    scaled = centred * lax.rsqrt(var + 1e-05)
    normed = (scaled * own_ref[:, 2 * width : 3 * width].astype(F32)).astype(BF16)
    w_copy.wait()
    pieces = out_sems.shape[0]
    count = cand_ref.shape[0] // pieces
    outs = []
    for index in range(pieces):
        span = slice(index * count, (index + 1) * count)
        result = cand_ref[span].astype(F32) + dot(normed[span], w_ref[...])
        out_ref[span] = result.astype(BF16)
        block = pl.ds(index * count, count)
        copy = pltpu.make_async_copy(out_ref.at[block], out_hbm.at[block], out_sems.at[index])
        copy.start()
        outs.append(copy)
    for copy in outs:
        copy.wait()


def tail(got, own, candidates, w_out):
    rows, width = candidates.shape
    inside = pl.BlockSpec(memory_space=pltpu.VMEM)
    return pl.pallas_call(
        tail_kernel,
        in_specs=[inside] * 3 + [pl.BlockSpec(memory_space=pl.ANY)],
        out_specs=pl.BlockSpec(memory_space=pl.ANY),
        out_shape=jax.ShapeDtypeStruct((rows, width), BF16),
        scratch_shapes=[
            pltpu.VMEM(w_out.shape, BF16),
            pltpu.VMEM((rows, width), BF16),
            pltpu.SemaphoreType.DMA((1,)),
            pltpu.SemaphoreType.DMA((2,)),
        ],
        compiler_params=params(50),
        cost_estimate=pl.CostEstimate(
            flops=2 * rows * width * (width + got.shape[0] * 8), bytes_accessed=6 << 20, transcendentals=rows
        ),
        name="tail",
    )(got, own, candidates, w_out)


def exchange(rows):
    tiles, pair, eight, half = rows.shape
    flat = rows.reshape(tiles * pair, eight, half)
    return lax.all_to_all(flat, "serve", split_axis=0, concat_axis=0, tiled=True).reshape(rows.shape)


def per_device(history, candidates, cand_user, hist_len, w_uvqk, w_out):
    users = lax.axis_size("serve")
    outgoing, place = front(cand_user, candidates, w_uvqk, users)
    outgoing, history, place = lax.optimization_barrier((outgoing, history, place))
    received = exchange(outgoing)
    info = jnp.concatenate([hist_len, lax.axis_index("rep").astype(jnp.int32)[None]])
    key, value = keys_vals(info, history, w_uvqk)
    key, value, place = lax.optimization_barrier((key, value, place))
    other_key, other_value = (lax.ppermute(half, "rep", [(0, 1), (1, 0)]) for half in (key, value))
    own = own_part(candidates, w_uvqk, place)
    received, own = lax.optimization_barrier((received, own))
    returned = exchange(attention(received, (key, other_key), (value, other_value)))
    return tail(returned, own, candidates, w_out)


def solution(mesh):
    placed = (
        P(("serve", "rep"), None),
        P(("serve", "rep"), None),
        P(("serve", "rep"), None),
        P("serve"),
        P(),
        P(),
    )
    return jax.shard_map(
        per_device, mesh=mesh, in_specs=placed, out_specs=P(("serve", "rep"), None), check_vma=False
    )
```

```python
import functools
import math

import jax
import jax.numpy as jnp
from jax import lax
from jax.experimental import pallas as pl
from jax.experimental.pallas import tpu as pltpu
from jax.sharding import PartitionSpec as P

HEADS = 8
CAP = 4
BF16 = jnp.bfloat16
F32 = jnp.float32


def silu(x):
    y = 0.5 * x
    return y + y * jnp.tanh(y)


def dot(a, b):
    return jnp.dot(a, b, preferred_element_type=F32)


def turn(matrix, identity):
    turned = lax.dot_general(matrix, identity, (((0,), (0,)), ((), ())), preferred_element_type=F32)
    return turned.astype(BF16)


def weave(first, second):
    low = lax.broadcasted_iota(jnp.int32, first.shape, 1) < 4
    even = jnp.where(low, first, pltpu.roll(second, 4, 1))
    odd = jnp.where(low, pltpu.roll(first, 4, 1), second)
    return even, odd


def params(limit=60):
    return pltpu.CompilerParams(vmem_limit_bytes=limit << 20)


def front_kernel(
    user_hbm, cand_hbm, w_hbm, out_hbm, place_hbm, user_ref, cand_ref, w_ref, out_ref, place_ref, in_sems, out_sems
):
    slots, rows = place_ref.shape
    users = slots // CAP
    width = cand_ref.shape[1]
    parts, depth, _ = w_ref.shape
    copies = [
        pltpu.make_async_copy(user_hbm, user_ref, in_sems.at[0]),
        pltpu.make_async_copy(cand_hbm, cand_ref, in_sems.at[1]),
    ]
    for index in range(parts):
        source = w_hbm.at[pl.ds(index * depth, depth), pl.ds(2 * width, width)]
        copies.append(pltpu.make_async_copy(source, w_ref.at[index], in_sems.at[2 + index]))
    for copy in copies:
        copy.start()

    copies[0].wait()
    ids = user_ref[...]
    one_hot = jnp.where(ids == lax.broadcasted_iota(jnp.int32, (users, rows), 0), 1.0, 0.0)
    earlier = jnp.where(
        lax.broadcasted_iota(jnp.int32, (rows, rows), 0)
        < lax.broadcasted_iota(jnp.int32, (rows, rows), 1),
        1.0,
        0.0,
    )
    before = dot(one_hot.astype(BF16), earlier.astype(BF16))
    rank = jnp.sum(before * one_hot, 0, keepdims=True).astype(jnp.int32)
    slot = ids * CAP + rank
    place = jnp.where(slot == lax.broadcasted_iota(jnp.int32, (slots, rows), 0), 1.0, 0.0).astype(BF16)
    place_ref[...] = place
    outs = [pltpu.make_async_copy(place_ref, place_hbm, out_sems.at[0])]
    outs[0].start()

    copies[1].wait()
    total = None
    for index in range(parts):
        copies[2 + index].wait()
        term = dot(cand_ref[:, index * depth : (index + 1) * depth], w_ref[index])
        total = term if total is None else total + term
    query = silu(total).astype(BF16)
    half = width // 2
    pieces = out_sems.shape[0] - 1
    count = slots // pieces
    tiles = count // 8
    for index in range(pieces):
        moved = dot(place[index * count : (index + 1) * count], query).reshape(tiles, 8, width)
        even, odd = weave(moved[:, :, :half], moved[:, :, half:])
        span = pl.ds(index * tiles, tiles)
        out_ref[span, 0] = even.astype(BF16)
        out_ref[span, 1] = odd.astype(BF16)
        copy = pltpu.make_async_copy(out_ref.at[span], out_hbm.at[span], out_sems.at[1 + index])
        copy.start()
        outs.append(copy)
    for copy in outs:
        copy.wait()


def front(cand_user, candidates, w_uvqk, users):
    rows, width = candidates.shape
    half = width // 2
    slots = users * CAP
    parts = 4
    pieces = 4
    whole = pl.BlockSpec(memory_space=pl.ANY)
    tiles = (slots // 8, 2, 8, half)
    return pl.pallas_call(
        front_kernel,
        in_specs=[whole] * 3,
        out_specs=[whole] * 2,
        out_shape=[
            jax.ShapeDtypeStruct(tiles, BF16),
            jax.ShapeDtypeStruct((slots, rows), BF16),
        ],
        scratch_shapes=[
            pltpu.VMEM((1, rows), jnp.int32),
            pltpu.VMEM((rows, width), BF16),
            pltpu.VMEM((parts, width // parts, width), BF16),
            pltpu.VMEM(tiles, BF16),
            pltpu.VMEM((slots, rows), BF16),
            pltpu.SemaphoreType.DMA((parts + 2,)),
            pltpu.SemaphoreType.DMA((pieces + 1,)),
        ],
        compiler_params=params(),
        cost_estimate=pl.CostEstimate(
            flops=2 * rows * width * (width + slots), bytes_accessed=5 << 20, transcendentals=rows * width
        ),
        name="front",
    )(cand_user.reshape(1, rows), candidates, w_uvqk)


def keys_vals_kernel(steps, info_ref, own_ref, w_ref, key_ref, value_ref):
    count = own_ref.shape[0]
    result = silu(dot(own_ref[...], w_ref[...]))

    @pl.when(pl.program_id(0) < steps)
    def _():
        row = lax.broadcasted_iota(jnp.int32, (count, count), 0)
        column = lax.broadcasted_iota(jnp.int32, (count, count), 1)
        identity = jnp.where(row == column, 1.0, 0.0).astype(BF16)
        key_ref[...] = turn(result.astype(BF16), identity)

    @pl.when(pl.program_id(0) >= steps)
    def _():
        event = info_ref[1] * count + lax.broadcasted_iota(jnp.int32, result.shape, 0)
        value = jnp.where(event < info_ref[0], result, 0.0).astype(BF16)
        head_size = value_ref.shape[2]
        for head in range(value_ref.shape[0]):
            value_ref[head] = value[:, head * head_size : (head + 1) * head_size]


def keys_vals(info, own, w_uvqk):
    count, width = own.shape
    block = min(256, width)
    steps = width // block
    return pl.pallas_call(
        functools.partial(keys_vals_kernel, steps),
        grid=(2 * steps,),
        in_specs=[
            pl.BlockSpec(memory_space=pltpu.SMEM),
            pl.BlockSpec((count, width), lambda j: (0, 0)),
            pl.BlockSpec((width, block), lambda j: (0, jnp.where(j < steps, 3 * steps + j, j))),
        ],
        out_specs=[
            pl.BlockSpec((block, count), lambda j: (jnp.minimum(j, steps - 1), 0)),
            pl.BlockSpec((HEADS // steps, count, width // HEADS), lambda j: (jnp.maximum(j - steps, 0), 0, 0)),
        ],
        out_shape=[
            jax.ShapeDtypeStruct((width, count), BF16),
            jax.ShapeDtypeStruct((HEADS, count, width // HEADS), BF16),
        ],
        compiler_params=params(),
        cost_estimate=pl.CostEstimate(
            flops=4 * count * width * width, bytes_accessed=7 << 20, transcendentals=2 * count * width
        ),
        name="keys_vals",
    )(info, own, w_uvqk)


def attention_kernel(
    got_ref, key0_hbm, key1_hbm, value0_hbm, value1_hbm, out_ref, key_ref, value_ref, in_sems
):
    tiles, _, _, half = got_ref.shape
    slots = tiles * 8
    head_size = 2 * half // HEADS
    pairs = HEADS // 2
    key_hbms, value_hbms = (key0_hbm, key1_hbm), (value0_hbm, value1_hbm)
    copies = {}
    count = key_hbms[0].shape[1]
    for pair in range(pairs):
        for head in (pair, pairs + pair):
            rows = pl.ds(head * head_size, head_size)
            copies[head] = []
            for part in range(2):
                span = pl.ds(part * count, count)
                sem = in_sems.at[head, part]
                copies[head].append(
                    pltpu.make_async_copy(key_hbms[part].at[rows], key_ref.at[head, :, span], sem.at[0])
                )
                copies[head].append(
                    pltpu.make_async_copy(value_hbms[part].at[head], value_ref.at[head, span], sem.at[1])
                )
            for copy in copies[head]:
                copy.start()
    scale = 0.5 / math.sqrt(head_size)
    for group in ((0,), (1, 2, 3)):
        for pair in group:
            for head in (pair, pairs + pair):
                for copy in copies[head]:
                    copy.wait()
        for pair in group:
            columns = pl.ds(pair * head_size, head_size)
            queries = weave(got_ref[:, 0, :, columns].astype(F32), got_ref[:, 1, :, columns].astype(F32))
            results = []
            for query, head in zip(queries, (pair, pairs + pair)):
                rows = query.reshape(slots, head_size).astype(BF16)
                y = dot(rows, key_ref[head]) * scale
                weights = (y + y * jnp.tanh(y)).astype(BF16)
                results.append(dot(weights, value_ref[head]).reshape(tiles, 8, head_size))
            even, odd = weave(*results)
            out_ref[:, 0, :, columns] = even.astype(BF16)
            out_ref[:, 1, :, columns] = odd.astype(BF16)


def attention(got, keys, values):
    tiles, _, _, half = got.shape
    slots = tiles * 8
    heads, count, head_size = values[0].shape
    events = 2 * count
    whole = pl.BlockSpec(memory_space=pl.ANY)
    return pl.pallas_call(
        attention_kernel,
        in_specs=[pl.BlockSpec(memory_space=pltpu.VMEM)] + [whole] * 4,
        out_specs=pl.BlockSpec(memory_space=pltpu.VMEM),
        out_shape=jax.ShapeDtypeStruct(got.shape, BF16),
        scratch_shapes=[
            pltpu.VMEM((heads, head_size, events), BF16),
            pltpu.VMEM((heads, events, head_size), BF16),
            pltpu.SemaphoreType.DMA((heads, 2, 2)),
        ],
        compiler_params=params(51),
        cost_estimate=pl.CostEstimate(
            flops=8 * slots * events * half,
            bytes_accessed=6 << 20,
            transcendentals=slots * events * heads,
        ),
        name="attention",
    )(got, *keys, *values)


def own_kernel(head_size, cand_ref, wg_ref, wv_ref, wq_ref, wk_ref, place_ref, out_ref):
    step = pl.program_id(0)
    block = wg_ref.shape[1]
    rows, width = cand_ref.shape
    slots = place_ref.shape[0]

    @pl.when(step == 0)
    def _():
        out_ref[:, 3 * width : 3 * width + slots] = place_ref[...].astype(F32).T.astype(BF16)

    cand = cand_ref[...]
    gate, value, query, key = (
        silu(dot(cand, ref[...])).astype(BF16) for ref in (wg_ref, wv_ref, wq_ref, wk_ref)
    )
    product = query.astype(F32) * key.astype(F32)
    value = value.astype(F32)
    terms = []
    for start in range(0, block, head_size):
        columns = slice(start, start + head_size)
        score = jnp.sum(product[:, columns], 1, keepdims=True) / math.sqrt(head_size)
        terms.append(silu(score) * value[:, columns])
    term = jnp.concatenate(terms, 1)
    high = term.astype(BF16)
    low = (term - high.astype(F32)).astype(BF16)
    for index, array in enumerate((high, low, gate)):
        start = pl.multiple_of(index * width + step * block, block)
        out_ref[:, pl.ds(start, block)] = array


def own_part(candidates, w_uvqk, place):
    rows, width = candidates.shape
    slots = place.shape[0]
    block = 256
    steps = width // block
    return pl.pallas_call(
        functools.partial(own_kernel, width // HEADS),
        grid=(steps,),
        in_specs=[
            pl.BlockSpec((rows, width), lambda j: (0, 0)),
            pl.BlockSpec((width, block), lambda j: (0, j)),
            pl.BlockSpec((width, block), lambda j: (0, steps + j)),
            pl.BlockSpec((width, block), lambda j: (0, 2 * steps + j)),
            pl.BlockSpec((width, block), lambda j: (0, 3 * steps + j)),
            pl.BlockSpec((slots, rows), lambda j: (0, 0)),
        ],
        out_specs=pl.BlockSpec((rows, 3 * width + slots), lambda j: (0, 0)),
        out_shape=jax.ShapeDtypeStruct((rows, 3 * width + slots), BF16),
        compiler_params=params(50),
        cost_estimate=pl.CostEstimate(
            flops=8 * rows * width * width, bytes_accessed=11 << 20, transcendentals=4 * rows * width
        ),
        name="own_part",
    )(candidates, w_uvqk, w_uvqk, w_uvqk, w_uvqk, place)


def tail_kernel(got_ref, own_ref, cand_ref, w_ref, out_hbm, out_ref, out_sems):
    tiles, _, _, half = got_ref.shape
    width = 2 * half
    slots = tiles * 8
    place = own_ref[:, 3 * width : 3 * width + slots]
    parts = weave(got_ref[:, 0].astype(F32), got_ref[:, 1].astype(F32))
    history = [dot(place, part.reshape(slots, half).astype(BF16)) for part in parts]
    term = own_ref[:, :width].astype(F32) + own_ref[:, width : 2 * width].astype(F32)
    attended = jnp.concatenate(history, 1) + term
    mean = jnp.sum(attended, 1, keepdims=True) / width
    centred = attended - mean
    var = jnp.sum(centred * centred, 1, keepdims=True) / width
    scaled = centred * lax.rsqrt(var + 1e-05)
    normed = (scaled * own_ref[:, 2 * width : 3 * width].astype(F32)).astype(BF16)
    pieces = out_sems.shape[0]
    count = cand_ref.shape[0] // pieces
    outs = []
    for index in range(pieces):
        span = slice(index * count, (index + 1) * count)
        result = cand_ref[span].astype(F32) + dot(normed[span], w_ref[...])
        out_ref[span] = result.astype(BF16)
        block = pl.ds(index * count, count)
        copy = pltpu.make_async_copy(out_ref.at[block], out_hbm.at[block], out_sems.at[index])
        copy.start()
        outs.append(copy)
    for copy in outs:
        copy.wait()


def tail(got, own, candidates, w_out):
    rows, width = candidates.shape
    inside = pl.BlockSpec(memory_space=pltpu.VMEM)
    return pl.pallas_call(
        tail_kernel,
        in_specs=[inside] * 4,
        out_specs=pl.BlockSpec(memory_space=pl.ANY),
        out_shape=jax.ShapeDtypeStruct((rows, width), BF16),
        scratch_shapes=[
            pltpu.VMEM((rows, width), BF16),
            pltpu.SemaphoreType.DMA((2,)),
        ],
        compiler_params=params(47),
        cost_estimate=pl.CostEstimate(
            flops=2 * rows * width * (width + got.shape[0] * 8), bytes_accessed=6 << 20, transcendentals=rows
        ),
        name="tail",
    )(got, own, candidates, w_out)


def exchange(rows):
    tiles, pair, eight, half = rows.shape
    flat = rows.reshape(tiles * pair, eight, half)
    return lax.all_to_all(flat, "serve", split_axis=0, concat_axis=0, tiled=True).reshape(rows.shape)


def per_device(history, candidates, cand_user, hist_len, w_uvqk, w_out):
    users = lax.axis_size("serve")
    outgoing, place = front(cand_user, candidates, w_uvqk, users)
    outgoing, history, place = lax.optimization_barrier((outgoing, history, place))
    received = exchange(outgoing)
    info = jnp.concatenate([hist_len, lax.axis_index("rep").astype(jnp.int32)[None]])
    key, value = keys_vals(info, history, w_uvqk)
    key, value, place = lax.optimization_barrier((key, value, place))
    other_key, other_value = (lax.ppermute(half, "rep", [(0, 1), (1, 0)]) for half in (key, value))
    own = own_part(candidates, w_uvqk, place)
    received, own = lax.optimization_barrier((received, own))
    returned = exchange(attention(received, (key, other_key), (value, other_value)))
    return tail(returned, own, candidates, w_out)


def solution(mesh):
    placed = (
        P(("serve", "rep"), None),
        P(("serve", "rep"), None),
        P(("serve", "rep"), None),
        P("serve"),
        P(),
        P(),
    )
    return jax.shard_map(
        per_device, mesh=mesh, in_specs=placed, out_specs=P(("serve", "rep"), None), check_vma=False
    )
```
